256 devices in a mesh: gx: 8 (over z_hi, core), gy: 32 (over x, z_lo, y).
Axes of the slice: x: 4, y: 4, z: 8 (z_hi: 4, z_lo: 2; z = z_hi * 2 + z_lo), core: 2. Of those that a mesh axis runs over, the one named last changes fastest.
Arguments:
- volume: float32 [192, 1024, 128], P('gx', 'gy'), may hold values from -12 to 12
Outputs:
- throat: float32 [192, 1024, 128], P('gx', 'gy')
The draws below stay inside these ranges and needn't reach their ends.
All inputs are finite; a program needn't handle non-finite values.
Results may differ from the reference program's by a relative error of at most 0.0003.
Values sent between devices are 32-bit elements; how exact they have to be, the bound alone decides.
No kernel may reach another device: no remote copies, remote signals or barrier semaphores. Data moves between devices by JAX's collectives and lax.ppermute only.
A program may use at most 64 MiB of HBM per device.

```python
import jax
import jax.numpy as jnp
from jax import lax

DEPTH = 128
NX = 192
NY = 1024


def draw_volume(key, part):
    key = jax.random.fold_in(key, 11)
    y_pos = jnp.arange(NY).astype(jnp.float32)
    contrast = (1.0 + 2.0 * y_pos / max(NY - 1, 1))[None, :, None]
    base = jax.random.truncated_normal(key, -4.0, 4.0, (NX, NY, DEPTH), jnp.float32)
    return base * contrast


def setup_inputs(seed: int = 0) -> dict:
    key_of = jax.random.split(jax.random.key(seed), 2)
    volume = draw_volume(jax.random.fold_in(key_of[1], 71), 0)
    return dict(volume=volume)


scale_list = (1.0, 2.0, 4.0, 8.0)
radius_list = (3, 6, 12, 24)

def derivative_taps(scale_sigma, radius):
    offsets = jnp.arange(-radius, radius + 1).astype(jnp.float32)
    bell = jnp.exp(-offsets * offsets / (2.0 * scale_sigma * scale_sigma))
    smooth_taps = bell / jnp.sum(bell)
    slope_taps = -offsets / (scale_sigma * scale_sigma) * smooth_taps
    curve_taps = (offsets * offsets / scale_sigma ** 4 - 1.0 / (scale_sigma * scale_sigma)) * smooth_taps
    return jnp.stack([smooth_taps, slope_taps, curve_taps])

def filter_along(stacked, chosen, radius, along_axis):
    n_chan = stacked.shape[0]
    tap_count = 2 * radius + 1
    kernel_shape = [n_chan, 1, 1, 1, 1]
    kernel_shape[2 + along_axis] = tap_count
    kernel = chosen[:, ::-1].reshape(kernel_shape)
    pad_pairs = [(0, 0), (0, 0), (0, 0)]
    pad_pairs[along_axis] = (radius, radius)
    result = lax.conv_general_dilated(stacked[None], kernel, (1, 1, 1), pad_pairs, dimension_numbers=('NCDHW', 'OIDHW', 'NCDHW'), feature_group_count=n_chan, precision=lax.Precision.HIGHEST)
    return result[0]

def invariants(hess_zz, hess_yz, hess_yy, hess_xz, hess_xy, hess_xx):
    trace_sum = hess_xx + hess_yy + hess_zz
    minors = hess_xx * hess_yy + hess_xx * hess_zz + hess_yy * hess_zz - hess_xy * hess_xy - hess_xz * hess_xz - hess_yz * hess_yz
    energy = hess_xx * hess_xx + hess_yy * hess_yy + hess_zz * hess_zz + 2.0 * (hess_xy * hess_xy + hess_xz * hess_xz + hess_yz * hess_yz)
    return (trace_sum, minors, energy)

def throat_score(trace_sum, minors, energy, peak):
    spread = 0.25 * peak + 1e-06
    guard = energy + 0.1 * spread
    return (1.0 - jnp.exp(-energy / (2.0 * spread))) * jnp.exp(-2.0 * minors * minors / (guard * guard)) * jax.nn.sigmoid(-4.0 * trace_sum / jnp.sqrt(guard))

def reference(volume):
    stats = []
    peaks = []
    for scale_sigma, radius in zip(scale_list, radius_list):
        kernel_taps = derivative_taps(scale_sigma, radius)
        along_x = filter_along(jnp.stack([volume, volume, volume]), kernel_taps, radius, 0)
        y_inputs = jnp.stack([along_x[0], along_x[0], along_x[0], along_x[1], along_x[1], along_x[2]])
        along_y = filter_along(y_inputs, kernel_taps[jnp.array([0, 1, 2, 0, 1, 0])], radius, 1)
        hessian = filter_along(along_y, kernel_taps[jnp.array([2, 1, 0, 1, 0, 0])], radius, 2) * (scale_sigma * scale_sigma)
        trace_sum, minors, energy = invariants(hessian[0], hessian[1], hessian[2], hessian[3], hessian[4], hessian[5])
        stats.append((trace_sum, minors, energy))
        peaks.append(jnp.max(energy))
    throat = throat_score(stats[0][0], stats[0][1], stats[0][2], peaks[0])
    for level in range(1, 4):
        throat = jnp.maximum(throat, throat_score(stats[level][0], stats[level][1], stats[level][2], peaks[level]))
    return throat
```

```python
import jax
import jax.numpy as jnp
import ml_dtypes
import numpy as np
from jax import lax
from jax.experimental import pallas as pl
from jax.experimental.pallas import tpu as pltpu
from jax.sharding import PartitionSpec as P

scale_list = (8.0, 4.0, 2.0, 1.0)
radius_list = (24, 12, 6, 3)
x_axes = ("zh", "core")
y_axes = ("x", "zl", "y")
rim = 24
tile_x, tile_y, depth = 24, 32, 128
wide_y = tile_y + 2 * rim
x_span = ((0, 80), (12, 48), (12, 48), (20, 32))
rows = tile_x * tile_y
z_rows = 96
score_rows = 192
mib = 1024 * 1024


def taps(scale, radius):
    t = np.arange(-radius, radius + 1).astype(np.float64)
    bell = np.exp(-t * t / (2.0 * scale * scale))
    w0 = bell / bell.sum()
    w1 = -t / (scale * scale) * w0
    w2 = (t * t / scale**4 - 1.0 / (scale * scale)) * w0
    return w0, w1, w2


def band(weights, radius, n_out, n_in, offset):
    lag = np.arange(n_out)[:, None] + offset - np.arange(n_in)[None, :]
    return np.where(np.abs(lag) <= radius, weights[np.clip(lag + radius, 0, 2 * radius)], 0.0)


def split(matrix):
    hi = matrix.astype(np.float32).astype(ml_dtypes.bfloat16)
    lo = (matrix - hi.astype(np.float64)).astype(np.float32).astype(ml_dtypes.bfloat16)
    return hi, lo


def constants():
    y_parts, x_parts, z_parts = [], [], []
    for scale, radius, (first, count) in zip(scale_list, radius_list, x_span):
        w = taps(scale, radius)
        y_parts += [band(v, radius, tile_y, wide_y, rim) for v in w]
        xb = np.concatenate([band(v, radius, tile_x, count, rim - first) for v in w])
        hi, lo = split(xb)
        x_parts.append(np.concatenate([hi, hi, lo], axis=1))
        for v in w:
            hi, lo = split(band(v * scale * scale, radius, depth, depth, 0).T)
            z_parts.append(
                np.concatenate(
                    [np.concatenate([hi, lo], axis=1), np.concatenate([hi, 0 * lo], axis=1)]
                )
            )
    hi, lo = split(np.concatenate(y_parts))
    y_all = np.concatenate([hi, hi, lo, np.zeros((hi.shape[0], 16), hi.dtype)], axis=1)
    return y_all, x_parts, np.stack(z_parts)


def halves(value):
    hi = value.astype(jnp.bfloat16)
    lo = (value - hi.astype(jnp.float32)).astype(jnp.bfloat16)
    return hi, lo


def dot(a, b):
    return jnp.dot(a, b, preferred_element_type=jnp.float32)


def filter_kernel(core_ref, *refs):
    sources, refs = refs[:8], refs[8:]
    wy, wx8, wx4, wx2, wx1, wz, stats_out, peaks, f8, f4, f2, f1, mixed, stats = refs[:14]
    held, in_sems, out_sems = refs[14:22], refs[22], refs[23]
    mid, pair, far, mid_lo, mid_hi, pair_y, far_lo, far_hi = held
    loads = [
        pltpu.make_async_copy(a, b, in_sems.at[i]) for i, (a, b) in enumerate(zip(sources, held))
    ]
    for i in (0, 3, 4, 1, 5, 2, 6, 7):
        loads[i].start()
    fields = (f8, f4, f2, f1)
    x_bands = (wx8, wx4, wx2, wx1)
    core = core_ref[0]
    f8[pl.ds(72 * 96, 8 * 96), :] = jnp.zeros((8 * 96, depth), jnp.float32)
    zeros16 = jnp.zeros((16, 2 * depth), jnp.bfloat16)

    def y_step(parts, plane, out_plane, levels):
        low, centre, high = parts(plane)
        both = jnp.concatenate([low, centre, high], axis=1)
        both = jnp.concatenate([both[0], both[1]], axis=1)
        hi, lo = halves(both)
        data = jnp.concatenate([hi, lo, hi, zeros16], axis=0)
        out = dot(wy[0 : 96 * levels, :], data)
        for level in range(levels):
            block = out[96 * level : 96 * level + 96]
            for k in range(2):
                at = pl.multiple_of((out_plane + k - x_span[level][0]) * 96, 96)
                fields[level][pl.ds(at, 96), :] = block[:, depth * k : depth * (k + 1)]

    def mid_parts(plane):
        at = pl.ds(plane, 2)
        return mid_lo[at], mid[at], mid_hi[at]

    def pair_parts(plane):
        at = pl.ds(plane, 2)
        return pair_y[at, 0:rim], pair[at], pair_y[at, rim : 2 * rim]

    def far_parts(plane):
        at = pl.ds(plane, 2)
        return far_lo[at], far[at], far_hi[at]

    def mid_body(i, carry):
        y_step(mid_parts, 2 * i, rim + 2 * i, 4)
        return carry

    for i in (0, 3, 4):
        loads[i].wait()
    lax.fori_loop(0, 12, mid_body, 0, unroll=2)

    sides = ((pair_parts, core, (1, 5)), (far_parts, 1 - core, (2, 6, 7)))
    for parts, before, needed in sides:
        for i in needed:
            loads[i].wait()
        for start, stop, levels in ((0, 2, 4), (2, 6, 3), (6, 12, 1)):

            def side_body(j, carry, parts=parts, before=before, levels=levels):
                i = j + before * (11 - 2 * j)
                y_step(parts, 2 * i, 2 * i + 48 * (1 - before), levels)
                return carry

            lax.fori_loop(start, stop, side_body, 0, unroll=2)

    peak_rows, stores = [], []
    for level in range(4):
        field, x_band = fields[level], x_bands[level]
        count = x_span[level][1]

        def x_body(yp, carry, field=field, x_band=x_band, count=count):
            at = pl.ds(pl.multiple_of(48 * yp, 48), 48)
            for f, first, outs in ((0, 0, 3), (1, 3, 2), (2, 5, 1)):
                pieces = [
                    field[pl.ds(32 * f + 2 * yp + k, count, stride=96), :] for k in range(2)
                ]
                hi, lo = halves(jnp.concatenate(pieces, axis=1))
                data = jnp.concatenate([hi, lo, hi], axis=0)
                out = dot(x_band[0 : 24 * outs, :], data)
                for k in range(outs):
                    u = out[24 * k : 24 * k + 24]
                    u = jnp.concatenate([u[:, :depth], u[:, depth:]], axis=0)
                    hi, lo = halves(u)
                    mixed[first + k, at, 0:depth] = hi
                    mixed[first + k, at, depth : 2 * depth] = lo
            return carry

        lax.fori_loop(0, tile_y // 2, x_body, 0, unroll=2)

        def z_body(c, best, level=level):
            at = pl.ds(pl.multiple_of(c * z_rows, z_rows), z_rows)

            def z_pass(order, chosen):
                data = jnp.concatenate([mixed[p, at, :] for p in chosen], axis=0)
                out = dot(data, wz[3 * level + order])
                out = out[:, :depth] + out[:, depth:]
                return [out[z_rows * k : z_rows * (k + 1)] for k in range(len(chosen))]

            (zz,) = z_pass(2, (0,))
            yz, xz = z_pass(1, (3, 1))
            yy, xy, xx = z_pass(0, (5, 4, 2))
            sq = xy * xy + xz * xz + yz * yz
            stats[3 * level, at, :] = xx + yy + zz
            stats[3 * level + 1, at, :] = xx * yy + (xx + yy) * zz - sq
            energy = xx * xx + yy * yy + zz * zz + 2.0 * sq
            stats[3 * level + 2, at, :] = energy
            return jnp.maximum(best, jnp.max(energy.reshape(z_rows // 8, 8, depth), axis=0))

        best = lax.fori_loop(0, rows // z_rows, z_body, jnp.zeros((8, depth), jnp.float32), unroll=2)
        at = pl.ds(3 * level, 3)
        stores.append(pltpu.make_async_copy(stats.at[at], stats_out.at[at], out_sems.at[level]))
        stores[-1].start()
        peak_rows.append(jnp.broadcast_to(jnp.max(best), (1, depth)))
    peaks[...] = jnp.concatenate(peak_rows + peak_rows, axis=0)
    for store in stores:
        store.wait()


def score_kernel(stats, peaks, throat, flat):
    step = pl.program_id(0)
    for c in range(score_rows // 24):
        at = pl.ds(24 * c, 24)
        best = None
        for level in range(4):
            trace_sum = stats[3 * level, at, :]
            minors = stats[3 * level + 1, at, :]
            energy = stats[3 * level + 2, at, :]
            spread = 0.25 * peaks[pl.ds(level, 1), :] + 1e-06
            guard = energy + 0.1 * spread
            ratio = minors / guard
            score = (
                (1.0 - jnp.exp(energy * (-0.5 / spread)))
                * jnp.exp(-2.0 * ratio * ratio)
                / (1.0 + jnp.exp(4.0 * trace_sum * lax.rsqrt(guard)))
            )
            best = score if best is None else jnp.maximum(best, score)
        flat[pl.ds(pl.multiple_of(step * score_rows + 24 * c, 8), 24), :] = best

    @pl.when(step == rows // score_rows - 1)
    def _():
        for i in range(tile_x):
            throat[i] = flat[pl.ds(i, tile_y, stride=tile_x), :]


def hbm(n):
    return [pl.BlockSpec(memory_space=pl.ANY)] * n


def vmem(n):
    return [pl.BlockSpec(memory_space=pltpu.VMEM)] * n


def filter_call(core, pieces, interpret=False):
    y_all, x_parts, z_all = constants()
    return pl.pallas_call(
        filter_kernel,
        out_shape=(
            jax.ShapeDtypeStruct((12, rows, depth), jnp.float32),
            jax.ShapeDtypeStruct((8, depth), jnp.float32),
        ),
        in_specs=[pl.BlockSpec(memory_space=pltpu.SMEM)] + hbm(8) + vmem(6),
        out_specs=(*hbm(1), *vmem(1)),
        scratch_shapes=[pltpu.VMEM((count * 96, depth), jnp.float32) for _, count in x_span]
        + [
            pltpu.VMEM((6, rows, 2 * depth), jnp.bfloat16),
            pltpu.VMEM((12, rows, depth), jnp.float32),
        ]
        + [pltpu.VMEM(piece.shape, jnp.float32) for piece in pieces]
        + [pltpu.SemaphoreType.DMA((8,)), pltpu.SemaphoreType.DMA((4,))],
        compiler_params=pltpu.CompilerParams(vmem_limit_bytes=40 * mib),
        interpret=interpret,
    )(core, *pieces, jnp.asarray(y_all), *[jnp.asarray(v) for v in x_parts], jnp.asarray(z_all))


def score_call(stats, peaks, interpret=False):
    return pl.pallas_call(
        score_kernel,
        out_shape=jax.ShapeDtypeStruct((tile_x, tile_y, depth), jnp.float32),
        grid=(rows // score_rows,),
        in_specs=[
            pl.BlockSpec((12, score_rows, depth), lambda i: (0, i, 0)),
            pl.BlockSpec((8, depth), lambda i: (0, 0)),
        ],
        out_specs=pl.BlockSpec((tile_x, tile_y, depth), lambda i: (0, 0, 0)),
        scratch_shapes=[pltpu.VMEM((rows, depth), jnp.float32)],
        compiler_params=pltpu.CompilerParams(vmem_limit_bytes=24 * mib),
        interpret=interpret,
    )(stats, peaks)


def global_max(block):
    for axis, step in (
        ("core", 1), ("y", 1), ("y", 2), ("x", 1), ("x", 2), ("zl", 1), ("zh", 1), ("zh", 2),
    ):
        pairs = [(i, i ^ step) for i in range(lax.axis_size(axis))]
        block = jnp.maximum(block, lax.ppermute(block, axis, pairs))
    return block


def per_device(volume):
    n_x, n_y = lax.axis_size(x_axes), lax.axis_size(y_axes)
    pair_perm = [(i, i ^ 1) for i in range(n_x)]
    far_perm = [(i, i + 1) for i in range(1, n_x - 1, 2)]
    far_perm += [(j, i) for i, j in far_perm]
    up = [(i, i + 1) for i in range(n_y - 1)]
    down = [(j, i) for i, j in up]
    tail, head = slice(tile_y - rim, tile_y), slice(0, rim)

    far = lax.ppermute(volume, x_axes, far_perm)
    mid_lo = lax.ppermute(volume[:, tail], y_axes, up)
    mid_hi = lax.ppermute(volume[:, head], y_axes, down)
    pair = lax.ppermute(volume, x_axes, pair_perm)
    far_lo = lax.ppermute(far[:, tail], y_axes, up)
    far_hi = lax.ppermute(far[:, head], y_axes, down)
    pair_y = lax.ppermute(jnp.concatenate([mid_lo, mid_hi], axis=1), x_axes, pair_perm)

    core = lax.axis_index("core").reshape(1)
    pieces = (volume, pair, far, mid_lo, mid_hi, pair_y, far_lo, far_hi)
    stats, peaks = filter_call(core, pieces)
    return score_call(stats, global_max(peaks))


def solution(mesh):
    fine = jax.sharding.Mesh(
        mesh.devices.reshape(4, 2, 4, 2, 4), ("zh", "core", "x", "zl", "y")
    )
    spec = P(x_axes, y_axes, None)
    return jax.shard_map(
        per_device, mesh=fine, in_specs=(spec,), out_specs=spec, check_vma=False
    )
```

```python
import jax
import jax.numpy as jnp
import ml_dtypes
import numpy as np
from jax import lax
from jax.experimental import pallas as pl
from jax.experimental.pallas import tpu as pltpu
from jax.sharding import PartitionSpec as P

scale_list = (8.0, 4.0, 2.0, 1.0)
radius_list = (24, 12, 6, 3)
x_axes = ("zh", "core")
y_axes = ("x", "zl", "y")
rim = 24
tile_x, tile_y, depth = 24, 32, 128
wide_y = tile_y + 2 * rim
x_span = ((0, 80), (12, 48), (12, 48), (20, 32))
rows = tile_x * tile_y
z_rows = 192
score_rows = 192
mib = 1024 * 1024


def taps(scale, radius):
    t = np.arange(-radius, radius + 1).astype(np.float64)
    bell = np.exp(-t * t / (2.0 * scale * scale))
    w0 = bell / bell.sum()
    w1 = -t / (scale * scale) * w0
    w2 = (t * t / scale**4 - 1.0 / (scale * scale)) * w0
    return w0, w1, w2


def band(weights, radius, n_out, n_in, offset):
    lag = np.arange(n_out)[:, None] + offset - np.arange(n_in)[None, :]
    return np.where(np.abs(lag) <= radius, weights[np.clip(lag + radius, 0, 2 * radius)], 0.0)


def split(matrix):
    hi = matrix.astype(np.float32).astype(ml_dtypes.bfloat16)
    lo = (matrix - hi.astype(np.float64)).astype(np.float32).astype(ml_dtypes.bfloat16)
    return hi, lo


def constants():
    y_parts, x_parts, z_parts = [], [], []
    for scale, radius, (first, count) in zip(scale_list, radius_list, x_span):
        w = taps(scale, radius)
        y_parts += [band(v, radius, tile_y, wide_y, rim) for v in w]
        xb = np.concatenate([band(v, radius, tile_x, count, rim - first) for v in w])
        hi, lo = split(xb)
        x_part = np.zeros((72, 2 * depth), hi.dtype)
        x_part[:, : 3 * count] = np.concatenate([hi, hi, lo], axis=1)
        x_parts.append(x_part)
        for v in w:
            hi, lo = split(band(v * scale * scale, radius, depth, depth, 0).T)
            z_parts.append(
                np.concatenate(
                    [np.concatenate([hi, lo], axis=1), np.concatenate([hi, 0 * lo], axis=1)]
                )
            )
    hi, lo = split(np.concatenate(y_parts))
    y_all = np.concatenate([hi, hi, lo, np.zeros((hi.shape[0], 16), hi.dtype)], axis=1)
    return y_all, np.stack(x_parts), np.stack(z_parts)


def halves(value):
    hi = value.astype(jnp.bfloat16)
    lo = (value - hi.astype(jnp.float32)).astype(jnp.bfloat16)
    return hi, lo


def dot(a, b):
    return jnp.dot(a, b, preferred_element_type=jnp.float32)


def filter_kernel(
    core_ref, mid_hbm, wy_hbm, wx_hbm, wz_hbm, pair, far, mid_lo, mid_hi, pair_y, far_lo, far_hi,
    stats_out, peaks, f8, f4, f2, f1, mixed, stats, mid, wy, wx, wz, in_sems, out_sems,
):
    loads = [
        pltpu.make_async_copy(a, b, in_sems.at[i])
        for i, (a, b) in enumerate(((mid_hbm, mid), (wy_hbm, wy), (wx_hbm, wx), (wz_hbm, wz)))
    ]
    for load in loads:
        load.start()
    fields = (f8, f4, f2, f1)
    core = core_ref[0]
    f8[pl.ds(72 * 96, 8 * 96), :] = jnp.zeros((8 * 96, depth), jnp.float32)
    zeros16 = jnp.zeros((16, 2 * depth), jnp.bfloat16)

    def y_step(parts, plane, out_plane, levels):
        low, centre, high = parts(plane)
        both = jnp.concatenate([low, centre, high], axis=1)
        both = jnp.concatenate([both[0], both[1]], axis=1)
        hi, lo = halves(both)
        data = jnp.concatenate([hi, lo, hi, zeros16], axis=0)
        out = dot(wy[0 : 96 * levels, :], data)
        for level in range(levels):
            block = out[96 * level : 96 * level + 96]
            for k in range(2):
                at = pl.multiple_of((out_plane + k - x_span[level][0]) * 96, 96)
                fields[level][pl.ds(at, 96), :] = block[:, depth * k : depth * (k + 1)]

    def mid_parts(plane):
        at = pl.ds(plane, 2)
        return mid_lo[at], mid[at], mid_hi[at]

    def pair_parts(plane):
        at = pl.ds(plane, 2)
        return pair_y[at, 0:rim], pair[at], pair_y[at, rim : 2 * rim]

    def far_parts(plane):
        at = pl.ds(plane, 2)
        return far_lo[at], far[at], far_hi[at]

    def mid_body(i, carry):
        y_step(mid_parts, 2 * i, rim + 2 * i, 4)
        return carry

    loads[0].wait()
    loads[1].wait()
    lax.fori_loop(0, 12, mid_body, 0, unroll=4)

    for parts, before in ((pair_parts, core), (far_parts, 1 - core)):
        for start, stop, levels in ((0, 2, 4), (2, 6, 3), (6, 10, 1), (10, 12, 1)):

            def side_body(j, carry, parts=parts, before=before, levels=levels):
                i = j + before * (11 - 2 * j)
                y_step(parts, 2 * i, 2 * i + 48 * (1 - before), levels)
                return carry

            lax.fori_loop(start, stop, side_body, 0, unroll=min(4, stop - start))

    loads[2].wait()
    loads[3].wait()
    lane = lax.broadcasted_iota(jnp.int32, (1, depth), 1)
    peak_row = jnp.zeros((1, depth), jnp.float32)
    stores = []
    for level in range(4):
        field = fields[level]
        count = x_span[level][1]

        def x_body(yp, carry, field=field, level=level, count=count):
            at = pl.ds(pl.multiple_of(48 * yp, 48), 48)
            for f, first, outs in ((0, 0, 3), (1, 3, 2), (2, 5, 1)):
                pieces = [
                    field[pl.ds(32 * f + 2 * yp + k, count, stride=96), :] for k in range(2)
                ]
                hi, lo = halves(jnp.concatenate(pieces, axis=1))
                data = jnp.concatenate([hi, lo, hi], axis=0)
                out = dot(wx[level, 0 : 24 * outs, 0 : 3 * count], data)
                for k in range(outs):
                    u = out[24 * k : 24 * k + 24]
                    u = jnp.concatenate([u[:, :depth], u[:, depth:]], axis=0)
                    hi, lo = halves(u)
                    mixed[first + k, at, 0:depth] = hi
                    mixed[first + k, at, depth : 2 * depth] = lo
            return carry

        lax.fori_loop(0, tile_y // 2, x_body, 0, unroll=4)

        def z_body(c, best, level=level):
            at = pl.ds(pl.multiple_of(c * z_rows, z_rows), z_rows)

            def z_pass(order, chosen):
                data = jnp.concatenate([mixed[p, at, :] for p in chosen], axis=0)
                out = dot(data, wz[3 * level + order])
                out = out[:, :depth] + out[:, depth:]
                return [out[z_rows * k : z_rows * (k + 1)] for k in range(len(chosen))]

            (zz,) = z_pass(2, (0,))
            yz, xz = z_pass(1, (3, 1))
            yy, xy, xx = z_pass(0, (5, 4, 2))
            sq = xy * xy + xz * xz + yz * yz
            stats[3 * level, at, :] = xx + yy + zz
            stats[3 * level + 1, at, :] = xx * yy + (xx + yy) * zz - sq
            energy = xx * xx + yy * yy + zz * zz + 2.0 * sq
            stats[3 * level + 2, at, :] = energy
            return jnp.maximum(best, jnp.max(energy.reshape(z_rows // 8, 8, depth), axis=0))

        best = lax.fori_loop(0, rows // z_rows, z_body, jnp.zeros((8, depth), jnp.float32))
        at = pl.ds(3 * level, 3)
        stores.append(pltpu.make_async_copy(stats.at[at], stats_out.at[at], out_sems.at[level]))
        stores[-1].start()
        peak_row = jnp.where(lane == level, jnp.max(best), peak_row)
    peaks[...] = peak_row
    for store in stores:
        store.wait()


def score_kernel(stats, all_peaks, throat, flat):
    step = pl.program_id(0)
    peaks = jnp.max(all_peaks[...], axis=0, keepdims=True)
    for c in range(score_rows // 24):
        at = pl.ds(24 * c, 24)
        best = None
        for level in range(4):
            trace_sum = stats[3 * level, at, :]
            minors = stats[3 * level + 1, at, :]
            energy = stats[3 * level + 2, at, :]
            spread = 0.25 * peaks[:, level : level + 1] + 1e-06
            guard = energy + 0.1 * spread
            ratio = minors / guard
            score = (
                (1.0 - jnp.exp(energy * (-0.5 / spread)))
                * jnp.exp(-2.0 * ratio * ratio)
                / (1.0 + jnp.exp(4.0 * trace_sum * lax.rsqrt(guard)))
            )
            best = score if best is None else jnp.maximum(best, score)
        flat[pl.ds(pl.multiple_of(step * score_rows + 24 * c, 8), 24), :] = best

    @pl.when(step == rows // score_rows - 1)
    def _():
        for i in range(tile_x):
            throat[i] = flat[pl.ds(i, tile_y, stride=tile_x), :]


def vmem(n):
    return [pl.BlockSpec(memory_space=pltpu.VMEM)] * n


def filter_call(core, pieces, interpret=False):
    weights = constants()
    held = [pltpu.VMEM((tile_x, tile_y, depth), jnp.float32)]
    held += [pltpu.VMEM(w.shape, jnp.bfloat16) for w in weights]
    return pl.pallas_call(
        filter_kernel,
        out_shape=(
            jax.ShapeDtypeStruct((12, rows, depth), jnp.float32),
            jax.ShapeDtypeStruct((1, depth), jnp.float32),
        ),
        in_specs=[pl.BlockSpec(memory_space=pltpu.SMEM)]
        + [pl.BlockSpec(memory_space=pltpu.HBM)] * 4
        + vmem(7),
        out_specs=(pl.BlockSpec(memory_space=pl.ANY), vmem(1)[0]),
        scratch_shapes=[pltpu.VMEM((count * 96, depth), jnp.float32) for _, count in x_span]
        + [
            pltpu.VMEM((6, rows, 2 * depth), jnp.bfloat16),
            pltpu.VMEM((12, rows, depth), jnp.float32),
        ]
        + held
        + [pltpu.SemaphoreType.DMA((4,)), pltpu.SemaphoreType.DMA((4,))],
        compiler_params=pltpu.CompilerParams(vmem_limit_bytes=40 * mib),
        interpret=interpret,
    )(core, pieces[0], *[jnp.asarray(w) for w in weights], *pieces[1:])


def score_call(stats, peaks, interpret=False):
    return pl.pallas_call(
        score_kernel,
        out_shape=jax.ShapeDtypeStruct((tile_x, tile_y, depth), jnp.float32),
        grid=(rows // score_rows,),
        in_specs=[
            pl.BlockSpec((12, score_rows, depth), lambda i: (0, i, 0)),
            pl.BlockSpec(peaks.shape, lambda i: (0, 0)),
        ],
        out_specs=pl.BlockSpec((tile_x, tile_y, depth), lambda i: (0, 0, 0)),
        scratch_shapes=[pltpu.VMEM((rows, depth), jnp.float32)],
        compiler_params=pltpu.CompilerParams(vmem_limit_bytes=24 * mib),
        interpret=interpret,
    )(stats, peaks)


def all_peaks(row):
    row = jnp.maximum(row, lax.ppermute(row, "core", [(0, 1), (1, 0)]))
    axes = ("zh", "x", "zl", "y")
    peers = lax.axis_size(axes)
    spread = jnp.broadcast_to(row[None], (peers, 1, depth))
    return lax.all_to_all(spread, axes, 0, 0, tiled=True).reshape(peers, depth)


def per_device(volume):
    n_x, n_y = lax.axis_size(x_axes), lax.axis_size(y_axes)
    pair_perm = [(i, i ^ 1) for i in range(n_x)]
    far_perm = [(i, i + 1) for i in range(1, n_x - 1, 2)]
    far_perm += [(j, i) for i, j in far_perm]
    up = [(i, i + 1) for i in range(n_y - 1)]
    down = [(j, i) for i, j in up]
    tail, head = slice(tile_y - rim, tile_y), slice(0, rim)

    far = lax.ppermute(volume, x_axes, far_perm)
    pair = lax.ppermute(volume, x_axes, pair_perm)
    own = volume
    mid_lo = lax.ppermute(own[:, tail], y_axes, up)
    mid_hi = lax.ppermute(own[:, head], y_axes, down)
    far, mid_lo, mid_hi = lax.optimization_barrier((far, mid_lo, mid_hi))
    far_lo = lax.ppermute(far[:, tail], y_axes, up)
    far_hi = lax.ppermute(far[:, head], y_axes, down)
    pair_y = lax.ppermute(jnp.concatenate([mid_lo, mid_hi], axis=1), x_axes, pair_perm)

    core = lax.axis_index("core").reshape(1)
    pieces = (volume, pair, far, mid_lo, mid_hi, pair_y, far_lo, far_hi)
    stats, peaks = filter_call(core, pieces)
    return score_call(stats, all_peaks(peaks))


def solution(mesh):
    fine = jax.sharding.Mesh(
        mesh.devices.reshape(4, 2, 4, 2, 4), ("zh", "core", "x", "zl", "y")
    )
    spec = P(x_axes, y_axes, None)
    return jax.shard_map(
        per_device, mesh=fine, in_specs=(spec,), out_specs=spec, check_vma=False
    )
```

```python
import jax
import jax.numpy as jnp
import ml_dtypes
import numpy as np
from jax import lax
from jax.experimental import pallas as pl
from jax.experimental.pallas import tpu as pltpu
from jax.sharding import PartitionSpec as P

scale_list = (8.0, 4.0, 2.0, 1.0)
radius_list = (24, 12, 6, 3)
x_axes = ("zh", "core")
y_axes = ("x", "zl", "y")
rim = 24
tile_x, tile_y, depth = 24, 32, 128
wide_y = tile_y + 2 * rim
near = (24, 12, 12, 4)
planes = (80, 48, 48, 32)
rows = tile_x * tile_y
z_rows = 192
pitch = 104
mib = 1024 * 1024
log2_e = float(np.log2(np.e))


def taps(scale, radius):
    t = np.arange(-radius, radius + 1).astype(np.float64)
    bell = np.exp(-t * t / (2.0 * scale * scale))
    w0 = bell / bell.sum()
    w1 = -t / (scale * scale) * w0
    w2 = (t * t / scale**4 - 1.0 / (scale * scale)) * w0
    return w0, w1, w2


def band(weights, radius, out_places, in_places):
    lag = out_places[:, None] - in_places[None, :]
    return np.where(np.abs(lag) <= radius, weights[np.clip(lag + radius, 0, 2 * radius)], 0.0)


def split(matrix):
    hi = matrix.astype(np.float32).astype(ml_dtypes.bfloat16)
    lo = (matrix - hi.astype(np.float64)).astype(np.float32).astype(ml_dtypes.bfloat16)
    return hi, lo


def x_places(core, level):
    n = near[level]
    after, before = 2 * rim + np.arange(n), rim - n + np.arange(n)
    sides = [before, after] if core else [after, before]
    padding = np.full(planes[level] - rim - 2 * n, 1000)
    return np.concatenate([rim + np.arange(tile_x)] + sides + [padding])


def constants():
    y_parts, z_parts = [], []
    x_all = np.zeros((2, 4, 3 * tile_x, 2 * depth), ml_dtypes.bfloat16)
    y_places = np.arange(wide_y)
    for level, (scale, radius) in enumerate(zip(scale_list, radius_list)):
        w = taps(scale, radius)
        y_parts += [band(v, radius, rim + np.arange(tile_y), y_places) for v in w]
        for core in range(2):
            places = x_places(core, level)
            hi, lo = split(
                np.concatenate([band(v, radius, rim + np.arange(tile_x), places) for v in w])
            )
            x_all[core, level, :, : 3 * len(places)] = np.concatenate([hi, hi, lo], axis=1)
        for v in w:
            hi, lo = split(band(v * scale * scale, radius, np.arange(depth), np.arange(depth)).T)
            z_parts.append(
                np.concatenate(
                    [np.concatenate([hi, lo], axis=1), np.concatenate([hi, 0 * lo], axis=1)]
                )
            )
    hi, lo = split(np.concatenate(y_parts))
    y_all = np.concatenate([hi, hi, lo, np.zeros((hi.shape[0], 16), hi.dtype)], axis=1)
    return y_all, x_all, np.stack(z_parts)


def halves(value):
    hi = value.astype(jnp.bfloat16)
    lo = (value - hi.astype(jnp.float32)).astype(jnp.bfloat16)
    return hi, lo


def dot(a, b):
    return jnp.dot(a, b, preferred_element_type=jnp.float32)


def y_step(fields, wy, parts, slots):
    both = jnp.concatenate(parts, axis=1)
    both = jnp.concatenate([both[0], both[1]], axis=1)
    hi, lo = halves(both)
    zeros = jnp.zeros((16, 2 * depth), jnp.bfloat16)
    out = dot(wy[0 : 96 * len(slots), :], jnp.concatenate([hi, lo, hi, zeros], axis=0))
    for level, slot in enumerate(slots):
        for k in range(2):
            at = pl.multiple_of((slot + k) * pitch, 8)
            block = out[96 * level : 96 * level + 96, depth * k : depth * (k + 1)]
            fields[level][pl.ds(at, 96), :] = block


def side_steps(fields, wy, parts, before, base):
    for start, stop, levels in ((0, 2, 4), (2, 6, 3), (6, 10, 1), (10, 12, 1)):

        def body(j, carry, levels=levels):
            plane = 2 * (j + before * (11 - 2 * j))
            slots = [base[v] + plane - (rim - near[v]) * before for v in range(levels)]
            y_step(fields, wy, parts(plane), slots)
            return carry

        lax.fori_loop(start, stop, body, 0, unroll=min(4, stop - start))


def early_kernel(mid, wy, wx, wz, mid_lo, mid_hi, g8, g4, g2, g1):
    def mid_body(i, carry):
        at = pl.ds(2 * i, 2)
        y_step((g8, g4, g2, g1), wy, [mid_lo[at], mid[at], mid_hi[at]], [2 * i] * 4)
        return carry

    lax.fori_loop(0, tile_x // 2, mid_body, 0, unroll=4)


def late_kernel(
    core_ref, wy, wx, wz, far, far_lo, far_hi, pair, pair_lo, pair_hi, g8, g4, g2, g1,
    stats, peaks, f8, f4, f2, f1, mixed,
):
    own_fields, fields = (g8, g4, g2, g1), (f8, f4, f2, f1)
    core = core_ref[0]
    f8[pl.ds(2 * rim * pitch, 8 * pitch), :] = jnp.zeros((8 * pitch, depth), jnp.float32)

    def pair_parts(plane):
        at = pl.ds(plane, 2)
        return [pair_lo[at], pair[at], pair_hi[at]]

    def far_parts(plane):
        at = pl.ds(plane, 2)
        return [far_lo[at], far[at], far_hi[at]]

    side_steps(fields, wy, pair_parts, core, [0] * 4)
    side_steps(fields, wy, far_parts, 1 - core, near)

    lane = lax.broadcasted_iota(jnp.int32, (1, depth), 1)
    peak_row = jnp.zeros((1, depth), jnp.float32)
    for level in range(4):
        own, field = own_fields[level], fields[level]
        count = planes[level]

        def x_body(yp, carry, own=own, field=field, level=level, count=count):
            at = pl.ds(pl.multiple_of(48 * yp, 48), 48)
            for f, first, outs in ((0, 0, 3), (1, 3, 2), (2, 5, 1)):
                pieces = [
                    [
                        own[pl.ds(32 * f + 2 * yp + k, tile_x, stride=pitch), :],
                        field[pl.ds(32 * f + 2 * yp + k, count - tile_x, stride=pitch), :],
                    ]
                    for k in range(2)
                ]
                pieces = [jnp.concatenate(piece, axis=0) for piece in pieces]
                hi, lo = halves(jnp.concatenate(pieces, axis=1))
                data = jnp.concatenate([hi, lo, hi], axis=0)
                out = dot(wx[core, level, 0 : 24 * outs, 0 : 3 * count], data)
                for k in range(outs):
                    u = out[24 * k : 24 * k + 24]
                    u = jnp.concatenate([u[:, :depth], u[:, depth:]], axis=0)
                    hi, lo = halves(u)
                    mixed[first + k, at, 0:depth] = hi
                    mixed[first + k, at, depth : 2 * depth] = lo
            return carry

        lax.fori_loop(0, tile_y // 2, x_body, 0, unroll=4)

        def z_body(c, best, level=level):
            at = pl.ds(pl.multiple_of(c * z_rows, z_rows), z_rows)

            def z_pass(order, chosen):
                data = jnp.concatenate([mixed[p, at, :] for p in chosen], axis=0)
                out = dot(data, wz[3 * level + order])
                out = out[:, :depth] + out[:, depth:]
                return [out[z_rows * k : z_rows * (k + 1)] for k in range(len(chosen))]

            (zz,) = z_pass(2, (0,))
            yz, xz = z_pass(1, (3, 1))
            yy, xy, xx = z_pass(0, (5, 4, 2))
            sq = xy * xy + xz * xz + yz * yz
            stats[3 * level, at, :] = xx + yy + zz
            stats[3 * level + 1, at, :] = xx * yy + (xx + yy) * zz - sq
            energy = xx * xx + yy * yy + zz * zz + 2.0 * sq
            stats[3 * level + 2, at, :] = energy
            return jnp.maximum(best, jnp.max(energy.reshape(z_rows // 8, 8, depth), axis=0))

        best = lax.fori_loop(0, rows // z_rows, z_body, jnp.zeros((8, depth), jnp.float32), unroll=2)
        peak_row = jnp.where(lane == level, jnp.max(best), peak_row)
    peaks[...] = peak_row


def score_kernel(stats, all_peaks, throat, flat):
    peaks = jnp.max(all_peaks[...], axis=0, keepdims=True)
    spreads = [0.25 * peaks[:, level : level + 1] + 1e-06 for level in range(4)]

    def body(c, carry):
        at = pl.ds(pl.multiple_of(c * 24, 24), 24)
        best = None
        for level, spread in enumerate(spreads):
            trace_sum = stats[3 * level, at, :]
            minors = stats[3 * level + 1, at, :]
            energy = stats[3 * level + 2, at, :]
            guard = energy + 0.1 * spread
            root = lax.rsqrt(guard)
            ratio = minors * root * root
            score = (
                (1.0 - jnp.exp2(energy * (-0.5 * log2_e / spread)))
                * jnp.exp2(ratio * ratio * (-2.0 * log2_e))
                * (1.0 - jnp.tanh(2.0 * trace_sum * root))
            )
            best = score if best is None else jnp.maximum(best, score)
        flat[at, :] = 0.5 * best
        return carry

    lax.fori_loop(0, rows // 24, body, 0, unroll=4)
    for i in range(tile_x):
        throat[i] = flat[pl.ds(i, tile_y, stride=tile_x), :]


def vmem(n):
    return [pl.BlockSpec(memory_space=pltpu.VMEM)] * n


def early_call(volume, mid_lo, mid_hi, weights, interpret=False):
    return pl.pallas_call(
        early_kernel,
        out_shape=[jax.ShapeDtypeStruct((tile_x * pitch, depth), jnp.float32)] * 4,
        in_specs=vmem(6),
        out_specs=vmem(4),
        compiler_params=pltpu.CompilerParams(vmem_limit_bytes=16 * mib),
        interpret=interpret,
    )(volume, *weights, mid_lo, mid_hi)


def late_call(core, weights, pieces, early, interpret=False):
    return pl.pallas_call(
        late_kernel,
        out_shape=(
            jax.ShapeDtypeStruct((12, rows, depth), jnp.float32),
            jax.ShapeDtypeStruct((1, depth), jnp.float32),
        ),
        in_specs=[pl.BlockSpec(memory_space=pltpu.SMEM)] + vmem(13),
        out_specs=tuple(vmem(2)),
        scratch_shapes=[
            pltpu.VMEM(((count - tile_x) * pitch, depth), jnp.float32) for count in planes
        ]
        + [pltpu.VMEM((6, rows, 2 * depth), jnp.bfloat16)],
        compiler_params=pltpu.CompilerParams(vmem_limit_bytes=24 * mib),
        interpret=interpret,
    )(core, *weights, *pieces, *early)


def score_call(stats, peaks, interpret=False):
    return pl.pallas_call(
        score_kernel,
        out_shape=jax.ShapeDtypeStruct((tile_x, tile_y, depth), jnp.float32),
        in_specs=vmem(2),
        out_specs=vmem(1)[0],
        scratch_shapes=[pltpu.VMEM((rows, depth), jnp.float32)],
        compiler_params=pltpu.CompilerParams(vmem_limit_bytes=8 * mib),
        interpret=interpret,
    )(stats, peaks)


def all_peaks(row):
    row = jnp.maximum(row, lax.ppermute(row, "core", [(0, 1), (1, 0)]))
    axes = ("zh", "x", "zl", "y")
    peers = lax.axis_size(axes)
    spread = jnp.broadcast_to(row[None], (peers, 1, depth))
    return lax.all_to_all(spread, axes, 0, 0, tiled=True).reshape(peers, depth)


def per_device(volume):
    n_x, n_y = lax.axis_size(x_axes), lax.axis_size(y_axes)
    pair_perm = [(i, i ^ 1) for i in range(n_x)]
    far_perm = [(i, i + 1) for i in range(1, n_x - 1, 2)]
    far_perm += [(j, i) for i, j in far_perm]
    up = [(i, i + 1) for i in range(n_y - 1)]
    down = [(j, i) for i, j in up]
    tail, head = slice(tile_y - rim, tile_y), slice(0, rim)

    core = lax.axis_index("core").reshape(1)
    volume, core = lax.optimization_barrier((volume, core))
    far = lax.ppermute(volume, x_axes, far_perm)
    mid_lo = lax.ppermute(volume[:, tail], y_axes, up)
    mid_hi = lax.ppermute(volume[:, head], y_axes, down)
    pair = lax.ppermute(volume, x_axes, pair_perm)
    far_lo, far_hi = far[:, tail], far[:, head]
    _, _, mid_lo, mid_hi = lax.optimization_barrier((far_lo, far_hi, mid_lo, mid_hi))
    far_lo = lax.ppermute(far_lo, y_axes, up)
    far_hi = lax.ppermute(far_hi, y_axes, down)
    weights = [jnp.asarray(w) for w in constants()]
    early = early_call(volume, mid_lo, mid_hi, weights)
    mid_lo, mid_hi, *early = lax.optimization_barrier((mid_lo, mid_hi, *early))
    pair_lo = lax.ppermute(mid_lo, x_axes, pair_perm)
    pair_hi = lax.ppermute(mid_hi, x_axes, pair_perm)
    pieces = (far, far_lo, far_hi, pair, pair_lo, pair_hi)
    stats, peaks = late_call(core, weights, pieces, early)
    return score_call(stats, all_peaks(peaks))


def solution(mesh):
    fine = jax.sharding.Mesh(
        mesh.devices.reshape(4, 2, 4, 2, 4), ("zh", "core", "x", "zl", "y")
    )
    spec = P(x_axes, y_axes, None)
    return jax.shard_map(
        per_device, mesh=fine, in_specs=(spec,), out_specs=spec, check_vma=False
    )
```

```python
import jax
import jax.numpy as jnp
import ml_dtypes
import numpy as np
from jax import lax
from jax.experimental import pallas as pl
from jax.experimental.pallas import tpu as pltpu
from jax.sharding import PartitionSpec as P

scale_list = (8.0, 4.0, 2.0, 1.0)
radius_list = (24, 12, 6, 3)
x_axes = ("zh", "core")
y_axes = ("x", "zl", "y")
rim = 24
tile_x, tile_y, depth = 24, 32, 128
wide_y = tile_y + 2 * rim
near = (24, 12, 12, 4)
planes = (80, 48, 48, 32)
rows = tile_x * tile_y
z_rows = 192
pitch = 104
mib = 1024 * 1024
log2_e = float(np.log2(np.e))


def taps(scale, radius):
    t = np.arange(-radius, radius + 1).astype(np.float64)
    bell = np.exp(-t * t / (2.0 * scale * scale))
    w0 = bell / bell.sum()
    w1 = -t / (scale * scale) * w0
    w2 = (t * t / scale**4 - 1.0 / (scale * scale)) * w0
    return w0, w1, w2


def band(weights, radius, out_places, in_places):
    lag = out_places[:, None] - in_places[None, :]
    return np.where(np.abs(lag) <= radius, weights[np.clip(lag + radius, 0, 2 * radius)], 0.0)


def split(matrix):
    hi = matrix.astype(np.float32).astype(ml_dtypes.bfloat16)
    lo = (matrix - hi.astype(np.float64)).astype(np.float32).astype(ml_dtypes.bfloat16)
    return hi, lo


def x_places(core, level):
    n = near[level]
    after, before = 2 * rim + np.arange(n), rim - n + np.arange(n)
    sides = [before, after] if core else [after, before]
    padding = np.full(planes[level] - rim - 2 * n, 1000)
    return np.concatenate([rim + np.arange(tile_x)] + sides + [padding])


def constants():
    y_parts, z_parts = [], []
    x_all = np.zeros((2, 4, 3 * tile_x, 2 * depth), ml_dtypes.bfloat16)
    y_places = np.arange(wide_y)
    for level, (scale, radius) in enumerate(zip(scale_list, radius_list)):
        w = taps(scale, radius)
        y_parts += [band(v, radius, rim + np.arange(tile_y), y_places) for v in w]
        for core in range(2):
            places = x_places(core, level)
            hi, lo = split(
                np.concatenate([band(v, radius, rim + np.arange(tile_x), places) for v in w])
            )
            x_all[core, level, :, : 3 * len(places)] = np.concatenate([hi, hi, lo], axis=1)
        for v in w:
            hi, lo = split(band(v * scale * scale, radius, np.arange(depth), np.arange(depth)).T)
            z_parts.append(
                np.concatenate(
                    [np.concatenate([hi, lo], axis=1), np.concatenate([hi, 0 * lo], axis=1)]
                )
            )
    hi, lo = split(np.concatenate(y_parts))
    y_all = np.concatenate([hi, hi, lo, np.zeros((hi.shape[0], 16), hi.dtype)], axis=1)
    return y_all, x_all, np.stack(z_parts)


def halves(value):
    hi = value.astype(jnp.bfloat16)
    lo = (value - hi.astype(jnp.float32)).astype(jnp.bfloat16)
    return hi, lo


def dot(a, b):
    return jnp.dot(a, b, preferred_element_type=jnp.float32)


def y_step(fields, wy, parts, slots):
    both = jnp.concatenate(parts, axis=1)
    both = jnp.concatenate([both[0], both[1]], axis=1)
    hi, lo = halves(both)
    zeros = jnp.zeros((16, 2 * depth), jnp.bfloat16)
    out = dot(wy[0 : 96 * len(slots), :], jnp.concatenate([hi, lo, hi, zeros], axis=0))
    for level, slot in enumerate(slots):
        for k in range(2):
            at = pl.multiple_of((slot + k) * pitch, 8)
            block = out[96 * level : 96 * level + 96, depth * k : depth * (k + 1)]
            fields[level][pl.ds(at, 96), :] = block


def side_steps(fields, wy, parts, before, base):
    for start, stop, levels in ((0, 2, 4), (2, 6, 3), (6, 10, 1), (10, 12, 1)):

        def body(j, carry, levels=levels):
            plane = 2 * (j + before * (11 - 2 * j))
            slots = [base[v] + plane - (rim - near[v]) * before for v in range(levels)]
            y_step(fields, wy, parts(plane), slots)
            return carry

        lax.fori_loop(start, stop, body, 0, unroll=min(4, stop - start))


def with_rims(upward, tile, mine, other):
    above = upward == 1
    return [jnp.where(above, other, mine), tile, jnp.where(above, mine, other)]


def early_kernel(place, mid, wy, wx, wz, got, passed, g8, g4, g2, g1):
    upward = place[1]

    def mid_body(i, carry):
        at, after = pl.ds(2 * i, 2), pl.ds(2 * i + tile_x, 2)
        parts = with_rims(upward, mid[at], got[at], passed[after])
        y_step((g8, g4, g2, g1), wy, parts, [2 * i] * 4)
        return carry

    lax.fori_loop(0, tile_x // 2, mid_body, 0, unroll=4)


def late_kernel(
    place, wy, wx, wz, far, far_got, far_passed, pair, got, passed, g8, g4, g2, g1,
    stats, peaks, f8, f4, f2, f1, mixed,
):
    own_fields, fields = (g8, g4, g2, g1), (f8, f4, f2, f1)
    core, upward = place[0], place[1]
    f8[pl.ds(2 * rim * pitch, 8 * pitch), :] = jnp.zeros((8 * pitch, depth), jnp.float32)

    def pair_parts(plane):
        at, after = pl.ds(plane, 2), pl.ds(plane + tile_x, 2)
        return with_rims(upward, pair[at], got[after], passed[at])

    def far_parts(plane):
        at = pl.ds(plane, 2)
        return with_rims(upward, far[at], far_got[at], far_passed[at])

    side_steps(fields, wy, pair_parts, core, [0] * 4)
    side_steps(fields, wy, far_parts, 1 - core, near)

    lane = lax.broadcasted_iota(jnp.int32, (1, depth), 1)
    peak_row = jnp.zeros((1, depth), jnp.float32)
    for level in range(4):
        own, field = own_fields[level], fields[level]
        count = planes[level]

        def x_body(yp, carry, own=own, field=field, level=level, count=count):
            at = pl.ds(pl.multiple_of(48 * yp, 48), 48)
            for f, first, outs in ((0, 0, 3), (1, 3, 2), (2, 5, 1)):
                pieces = [
                    [
                        own[pl.ds(32 * f + 2 * yp + k, tile_x, stride=pitch), :],
                        field[pl.ds(32 * f + 2 * yp + k, count - tile_x, stride=pitch), :],
                    ]
                    for k in range(2)
                ]
                pieces = [jnp.concatenate(piece, axis=0) for piece in pieces]
                hi, lo = halves(jnp.concatenate(pieces, axis=1))
                data = jnp.concatenate([hi, lo, hi], axis=0)
                out = dot(wx[core, level, 0 : 24 * outs, 0 : 3 * count], data)
                for k in range(outs):
                    u = out[24 * k : 24 * k + 24]
                    u = jnp.concatenate([u[:, :depth], u[:, depth:]], axis=0)
                    hi, lo = halves(u)
                    mixed[first + k, at, 0:depth] = hi
                    mixed[first + k, at, depth : 2 * depth] = lo
            return carry

        lax.fori_loop(0, tile_y // 2, x_body, 0, unroll=4)

        def z_body(c, best, level=level):
            at = pl.ds(pl.multiple_of(c * z_rows, z_rows), z_rows)

            def z_pass(order, chosen):
                data = jnp.concatenate([mixed[p, at, :] for p in chosen], axis=0)
                out = dot(data, wz[3 * level + order])
                out = out[:, :depth] + out[:, depth:]
                return [out[z_rows * k : z_rows * (k + 1)] for k in range(len(chosen))]

            (zz,) = z_pass(2, (0,))
            yz, xz = z_pass(1, (3, 1))
            yy, xy, xx = z_pass(0, (5, 4, 2))
            sq = xy * xy + xz * xz + yz * yz
            stats[3 * level, at, :] = xx + yy + zz
            stats[3 * level + 1, at, :] = xx * yy + (xx + yy) * zz - sq
            energy = xx * xx + yy * yy + zz * zz + 2.0 * sq
            stats[3 * level + 2, at, :] = energy
            return jnp.maximum(best, jnp.max(energy.reshape(z_rows // 8, 8, depth), axis=0))

        best = lax.fori_loop(0, rows // z_rows, z_body, jnp.zeros((8, depth), jnp.float32), unroll=2)
        peak_row = jnp.where(lane == level, jnp.max(best), peak_row)
    peaks[...] = peak_row


def score_kernel(stats, all_peaks, throat, flat):
    peaks = jnp.max(all_peaks[...], axis=0, keepdims=True)
    spreads = [0.25 * peaks[:, level : level + 1] + 1e-06 for level in range(4)]

    def body(c, carry):
        at = pl.ds(pl.multiple_of(c * 24, 24), 24)
        best = None
        for level, spread in enumerate(spreads):
            trace_sum = stats[3 * level, at, :]
            minors = stats[3 * level + 1, at, :]
            energy = stats[3 * level + 2, at, :]
            guard = energy + 0.1 * spread
            root = lax.rsqrt(guard)
            ratio = minors * root * root
            score = (
                (1.0 - jnp.exp2(energy * (-0.5 * log2_e / spread)))
                * jnp.exp2(ratio * ratio * (-2.0 * log2_e))
                * (1.0 - jnp.tanh(2.0 * trace_sum * root))
            )
            best = score if best is None else jnp.maximum(best, score)
        flat[at, :] = 0.5 * best
        return carry

    lax.fori_loop(0, rows // 24, body, 0, unroll=4)
    for i in range(tile_x):
        throat[i] = flat[pl.ds(i, tile_y, stride=tile_x), :]


def vmem(n):
    return [pl.BlockSpec(memory_space=pltpu.VMEM)] * n


def early_call(place, volume, got, passed, weights, interpret=False):
    return pl.pallas_call(
        early_kernel,
        out_shape=[jax.ShapeDtypeStruct((tile_x * pitch, depth), jnp.float32)] * 4,
        in_specs=[pl.BlockSpec(memory_space=pltpu.SMEM)] + vmem(6),
        out_specs=vmem(4),
        compiler_params=pltpu.CompilerParams(vmem_limit_bytes=16 * mib),
        interpret=interpret,
    )(place, volume, *weights, got, passed)


def late_call(place, weights, pieces, early, interpret=False):
    return pl.pallas_call(
        late_kernel,
        out_shape=(
            jax.ShapeDtypeStruct((12, rows, depth), jnp.float32),
            jax.ShapeDtypeStruct((1, depth), jnp.float32),
        ),
        in_specs=[pl.BlockSpec(memory_space=pltpu.SMEM)] + vmem(13),
        out_specs=tuple(vmem(2)),
        scratch_shapes=[
            pltpu.VMEM(((count - tile_x) * pitch, depth), jnp.float32) for count in planes
        ]
        + [pltpu.VMEM((6, rows, 2 * depth), jnp.bfloat16)],
        compiler_params=pltpu.CompilerParams(vmem_limit_bytes=24 * mib),
        interpret=interpret,
    )(place, *weights, *pieces, *early)


def score_call(stats, peaks, interpret=False):
    return pl.pallas_call(
        score_kernel,
        out_shape=jax.ShapeDtypeStruct((tile_x, tile_y, depth), jnp.float32),
        in_specs=vmem(2),
        out_specs=vmem(1)[0],
        scratch_shapes=[pltpu.VMEM((rows, depth), jnp.float32)],
        compiler_params=pltpu.CompilerParams(vmem_limit_bytes=8 * mib),
        interpret=interpret,
    )(stats, peaks)


def all_peaks(row):
    row = jnp.maximum(row, lax.ppermute(row, "core", [(0, 1), (1, 0)]))
    axes = ("zh", "x", "zl", "y")
    peers = lax.axis_size(axes)
    spread = jnp.broadcast_to(row[None], (peers, 1, depth))
    return lax.all_to_all(spread, axes, 0, 0, tiled=True).reshape(peers, depth)


def per_device(volume):
    n_x, n_y = lax.axis_size(x_axes), lax.axis_size(y_axes)
    pair_perm = [(i, i ^ 1) for i in range(n_x)]
    far_perm = [(i, i + 1) for i in range(1, n_x - 1, 2)]
    far_perm += [(j, i) for i, j in far_perm]
    trade = [(i, i ^ 1) for i in range(n_y)]
    trade += [(n_y + i, n_y + i + 1) for i in range(1, n_y - 1, 2)]
    trade += [(n_y + i + 1, n_y + i) for i in range(1, n_y - 1, 2)]

    core = lax.axis_index("core")
    upward = 1 - (core ^ (lax.axis_index("y") & 1))
    place = jnp.stack([core, upward]).astype(jnp.int32)
    volume, place, above, below = lax.optimization_barrier(
        (volume, place, upward == 1, upward == 0)
    )

    def edges(tile, towards):
        return jnp.where(towards, tile[:, tile_y - rim :], tile[:, :rim])

    def swap(value):
        return lax.ppermute(value, x_axes, pair_perm)

    far = lax.ppermute(volume, x_axes, far_perm)
    pair = swap(volume)
    rims = jnp.concatenate([edges(volume, above), edges(pair, above)], axis=0)
    got = lax.ppermute(rims, ("core",) + y_axes, trade)
    _, far = lax.optimization_barrier((rims, far))
    far_rims = jnp.concatenate([edges(far, above), swap(edges(far, below))], axis=0)
    _, got = lax.optimization_barrier((far_rims, got))
    far_got = lax.ppermute(far_rims, ("core",) + y_axes, trade)
    passed = swap(got)
    weights = [jnp.asarray(w) for w in constants()]
    early = early_call(place, volume, got, passed, weights)
    *early, far_got = lax.optimization_barrier((*early, far_got))
    far_passed = swap(far_got[tile_x:])
    pieces = (far, far_got, far_passed, pair, got, passed)
    stats, peaks = late_call(place, weights, pieces, early)
    return score_call(stats, all_peaks(peaks))


def solution(mesh):
    fine = jax.sharding.Mesh(
        mesh.devices.reshape(4, 2, 4, 2, 4), ("zh", "core", "x", "zl", "y")
    )
    spec = P(x_axes, y_axes, None)
    return jax.shard_map(
        per_device, mesh=fine, in_specs=(spec,), out_specs=spec, check_vma=False
    )
```

```python
import jax
import jax.numpy as jnp
import ml_dtypes
import numpy as np
from jax import lax
from jax.experimental import pallas as pl
from jax.experimental.pallas import tpu as pltpu
from jax.sharding import PartitionSpec as P

scale_list = (8.0, 4.0, 2.0, 1.0)
radius_list = (24, 12, 6, 3)
x_axes = ("zh", "core")
y_axes = ("x", "zl", "y")
rim = 24
tile_x, tile_y, depth = 24, 32, 128
wide_y = tile_y + 2 * rim
near = (24, 12, 12, 4)
planes = (80, 48, 48, 32)
rows = tile_x * tile_y
z_rows = 192
pitch = 104
mib = 1024 * 1024
log2_e = float(np.log2(np.e))


def taps(scale, radius):
    t = np.arange(-radius, radius + 1).astype(np.float64)
    bell = np.exp(-t * t / (2.0 * scale * scale))
    w0 = bell / bell.sum()
    w1 = -t / (scale * scale) * w0
    w2 = (t * t / scale**4 - 1.0 / (scale * scale)) * w0
    return w0, w1, w2


def band(weights, radius, out_places, in_places):
    lag = out_places[:, None] - in_places[None, :]
    return np.where(np.abs(lag) <= radius, weights[np.clip(lag + radius, 0, 2 * radius)], 0.0)


def split(matrix):
    hi = matrix.astype(np.float32).astype(ml_dtypes.bfloat16)
    lo = (matrix - hi.astype(np.float64)).astype(np.float32).astype(ml_dtypes.bfloat16)
    return hi, lo


def x_places(core, level):
    n = near[level]
    after, before = 2 * rim + np.arange(n), rim - n + np.arange(n)
    sides = [before, after] if core else [after, before]
    padding = np.full(planes[level] - rim - 2 * n, 1000)
    return np.concatenate([rim + np.arange(tile_x)] + sides + [padding])


def constants():
    y_parts, z_parts = [], []
    x_all = np.zeros((2, 4, 3 * tile_x, 2 * depth), ml_dtypes.bfloat16)
    y_places = np.arange(wide_y)
    for level, (scale, radius) in enumerate(zip(scale_list, radius_list)):
        w = taps(scale, radius)
        y_parts += [band(v, radius, rim + np.arange(tile_y), y_places) for v in w]
        for core in range(2):
            places = x_places(core, level)
            hi, lo = split(
                np.concatenate([band(v, radius, rim + np.arange(tile_x), places) for v in w])
            )
            x_all[core, level, :, : 3 * len(places)] = np.concatenate([hi, hi, lo], axis=1)
        for v in w:
            hi, lo = split(band(v * scale * scale, radius, np.arange(depth), np.arange(depth)).T)
            z_parts.append(
                np.concatenate(
                    [np.concatenate([hi, lo], axis=1), np.concatenate([hi, 0 * lo], axis=1)]
                )
            )
    hi, lo = split(np.concatenate(y_parts))
    y_all = np.concatenate([hi, hi, lo, np.zeros((hi.shape[0], 16), hi.dtype)], axis=1)
    return y_all, x_all, np.stack(z_parts)


def halves(value):
    hi = value.astype(jnp.bfloat16)
    lo = (value - hi.astype(jnp.float32)).astype(jnp.bfloat16)
    return hi, lo


def dot(a, b):
    return jnp.dot(a, b, preferred_element_type=jnp.float32)


def y_step(fields, wy, parts, slots):
    both = jnp.concatenate(parts, axis=1)
    both = jnp.concatenate([both[0], both[1]], axis=1)
    hi, lo = halves(both)
    zeros = jnp.zeros((16, 2 * depth), jnp.bfloat16)
    out = dot(wy[0 : 96 * len(slots), :], jnp.concatenate([hi, lo, hi, zeros], axis=0))
    for level, slot in enumerate(slots):
        for k in range(2):
            at = pl.multiple_of((slot + k) * pitch, 8)
            block = out[96 * level : 96 * level + 96, depth * k : depth * (k + 1)]
            fields[level][pl.ds(at, 96), :] = block


def side_steps(fields, wy, parts, before, base):
    for start, stop, levels in ((0, 2, 4), (2, 6, 3), (6, 10, 1), (10, 12, 1)):

        def body(j, carry, levels=levels):
            plane = 2 * (j + before * (11 - 2 * j))
            slots = [base[v] + plane - (rim - near[v]) * before for v in range(levels)]
            y_step(fields, wy, parts(plane), slots)
            return carry

        lax.fori_loop(start, stop, body, 0, unroll=min(4, stop - start))


def by_parity(place, step, near_rim, wrap_rim):
    for odd, rims in ((0, (wrap_rim, near_rim)), (1, (near_rim, wrap_rim))):

        @pl.when(place[1] == odd)
        def _(rims=rims):
            step(*rims)


def early_kernel(place, mid, wy, wx, wz, mid_near, mid_wrap, g8, g4, g2, g1):
    def step(low, high):
        def body(i, carry):
            at = pl.ds(2 * i, 2)
            y_step((g8, g4, g2, g1), wy, [low[at], mid[at], high[at]], [2 * i] * 4)
            return carry

        lax.fori_loop(0, tile_x // 2, body, 0, unroll=4)

    by_parity(place, step, mid_near, mid_wrap)


def late_kernel(
    place, wy, wx, wz, far, far_near, far_wrap, pair, pair_near, pair_wrap, g8, g4, g2, g1,
    stats, peaks, f8, f4, f2, f1, mixed,
):
    own_fields, fields = (g8, g4, g2, g1), (f8, f4, f2, f1)
    core = place[0]
    f8[pl.ds(2 * rim * pitch, 8 * pitch), :] = jnp.zeros((8 * pitch, depth), jnp.float32)

    def side(tile, before, base):
        def step(low, high):
            def parts(plane):
                at = pl.ds(plane, 2)
                return [low[at], tile[at], high[at]]

            side_steps(fields, wy, parts, before, base)

        return step

    by_parity(place, side(pair, core, [0] * 4), pair_near, pair_wrap)
    by_parity(place, side(far, 1 - core, near), far_near, far_wrap)

    lane = lax.broadcasted_iota(jnp.int32, (1, depth), 1)
    peak_row = jnp.zeros((1, depth), jnp.float32)
    for level in range(4):
        own, field = own_fields[level], fields[level]
        count = planes[level]

        def x_body(yp, carry, own=own, field=field, level=level, count=count):
            at = pl.ds(pl.multiple_of(48 * yp, 48), 48)
            for f, first, outs in ((0, 0, 3), (1, 3, 2), (2, 5, 1)):
                pieces = [
                    [
                        own[pl.ds(32 * f + 2 * yp + k, tile_x, stride=pitch), :],
                        field[pl.ds(32 * f + 2 * yp + k, count - tile_x, stride=pitch), :],
                    ]
                    for k in range(2)
                ]
                pieces = [jnp.concatenate(piece, axis=0) for piece in pieces]
                hi, lo = halves(jnp.concatenate(pieces, axis=1))
                data = jnp.concatenate([hi, lo, hi], axis=0)
                out = dot(wx[core, level, 0 : 24 * outs, 0 : 3 * count], data)
                for k in range(outs):
                    u = out[24 * k : 24 * k + 24]
                    u = jnp.concatenate([u[:, :depth], u[:, depth:]], axis=0)
                    hi, lo = halves(u)
                    mixed[first + k, at, 0:depth] = hi
                    mixed[first + k, at, depth : 2 * depth] = lo
            return carry

        lax.fori_loop(0, tile_y // 2, x_body, 0, unroll=8)

        def z_body(c, best, level=level):
            at = pl.ds(pl.multiple_of(c * z_rows, z_rows), z_rows)

            def z_pass(order, chosen):
                data = jnp.concatenate([mixed[p, at, :] for p in chosen], axis=0)
                out = dot(data, wz[3 * level + order])
                out = out[:, :depth] + out[:, depth:]
                return [out[z_rows * k : z_rows * (k + 1)] for k in range(len(chosen))]

            (zz,) = z_pass(2, (0,))
            yz, xz = z_pass(1, (3, 1))
            yy, xy, xx = z_pass(0, (5, 4, 2))
            sq = xy * xy + xz * xz + yz * yz
            stats[3 * level, at, :] = xx + yy + zz
            stats[3 * level + 1, at, :] = xx * yy + (xx + yy) * zz - sq
            energy = xx * xx + yy * yy + zz * zz + 2.0 * sq
            stats[3 * level + 2, at, :] = energy
            return jnp.maximum(best, jnp.max(energy.reshape(z_rows // 8, 8, depth), axis=0))

        best = lax.fori_loop(0, rows // z_rows, z_body, jnp.zeros((8, depth), jnp.float32), unroll=2)
        peak_row = jnp.where(lane == level, jnp.max(best), peak_row)
    peaks[...] = peak_row


def score_kernel(stats, all_peaks, throat, flat):
    peaks = jnp.max(all_peaks[...], axis=0, keepdims=True)
    spreads = [0.25 * peaks[:, level : level + 1] + 1e-06 for level in range(4)]

    def body(c, carry):
        at = pl.ds(pl.multiple_of(c * 24, 24), 24)
        best = None
        for level, spread in enumerate(spreads):
            trace_sum = stats[3 * level, at, :]
            minors = stats[3 * level + 1, at, :]
            energy = stats[3 * level + 2, at, :]
            guard = energy + 0.1 * spread
            root = lax.rsqrt(guard)
            ratio = minors * root * root
            score = (
                (1.0 - jnp.exp2(energy * (-0.5 * log2_e / spread)))
                * jnp.exp2(ratio * ratio * (-2.0 * log2_e))
                * (1.0 - jnp.tanh(2.0 * trace_sum * root))
            )
            best = score if best is None else jnp.maximum(best, score)
        flat[at, :] = 0.5 * best
        return carry

    lax.fori_loop(0, rows // 24, body, 0, unroll=4)
    for i in range(tile_x):
        throat[i] = flat[pl.ds(i, tile_y, stride=tile_x), :]


def vmem(n):
    return [pl.BlockSpec(memory_space=pltpu.VMEM)] * n


def early_call(place, volume, mid_near, mid_wrap, weights, interpret=False):
    return pl.pallas_call(
        early_kernel,
        out_shape=[jax.ShapeDtypeStruct((tile_x * pitch, depth), jnp.float32)] * 4,
        in_specs=[pl.BlockSpec(memory_space=pltpu.SMEM)] + vmem(6),
        out_specs=vmem(4),
        compiler_params=pltpu.CompilerParams(vmem_limit_bytes=16 * mib),
        interpret=interpret,
    )(place, volume, *weights, mid_near, mid_wrap)


def late_call(place, weights, pieces, early, interpret=False):
    return pl.pallas_call(
        late_kernel,
        out_shape=(
            jax.ShapeDtypeStruct((12, rows, depth), jnp.float32),
            jax.ShapeDtypeStruct((1, depth), jnp.float32),
        ),
        in_specs=[pl.BlockSpec(memory_space=pltpu.SMEM)] + vmem(13),
        out_specs=tuple(vmem(2)),
        scratch_shapes=[
            pltpu.VMEM(((count - tile_x) * pitch, depth), jnp.float32) for count in planes
        ]
        + [pltpu.VMEM((6, rows, 2 * depth), jnp.bfloat16)],
        compiler_params=pltpu.CompilerParams(vmem_limit_bytes=24 * mib),
        interpret=interpret,
    )(place, *weights, *pieces, *early)


def score_call(stats, peaks, interpret=False):
    return pl.pallas_call(
        score_kernel,
        out_shape=jax.ShapeDtypeStruct((tile_x, tile_y, depth), jnp.float32),
        in_specs=vmem(2),
        out_specs=vmem(1)[0],
        scratch_shapes=[pltpu.VMEM((rows, depth), jnp.float32)],
        compiler_params=pltpu.CompilerParams(vmem_limit_bytes=8 * mib),
        interpret=interpret,
    )(stats, peaks)


def all_peaks(row):
    axes = x_axes + y_axes
    peers = lax.axis_size(axes)
    spread = jnp.broadcast_to(row[None], (peers, 1, depth))
    return lax.all_to_all(spread, axes, 0, 0, tiled=True).reshape(peers, depth)


def per_device(volume):
    n_x, n_y = lax.axis_size(x_axes), lax.axis_size(y_axes)
    pair_perm = [(i, i ^ 1) for i in range(n_x)]
    far_perm = [(i, i + 1) for i in range(1, n_x - 1, 2)]
    far_perm += [(j, i) for i, j in far_perm]
    near_perm = [(i, i ^ 1) for i in range(n_y)]
    wrap_perm = [(i, i + 1) for i in range(1, n_y - 1, 2)]
    wrap_perm += [(j, i) for i, j in wrap_perm]

    odd = lax.axis_index("y") & 1
    place = jnp.stack([lax.axis_index("core"), odd]).astype(jnp.int32)
    volume, place, is_odd, is_even = lax.optimization_barrier((volume, place, odd == 1, odd == 0))

    def edge(tile, top):
        return jnp.where(top, tile[:, tile_y - rim :], tile[:, :rim])

    far = lax.ppermute(volume, x_axes, far_perm)
    mid_wrap = lax.ppermute(edge(volume, is_odd), y_axes, wrap_perm)
    mid_near = lax.ppermute(edge(volume, is_even), y_axes, near_perm)
    pair = lax.ppermute(volume, x_axes, pair_perm)
    far_wrap, far_near = edge(far, is_odd), edge(far, is_even)
    _, _, mid_wrap, mid_near = lax.optimization_barrier((far_wrap, far_near, mid_wrap, mid_near))
    far_wrap = lax.ppermute(far_wrap, y_axes, wrap_perm)
    far_near = lax.ppermute(far_near, y_axes, near_perm)
    weights = [jnp.asarray(w) for w in constants()]
    early = early_call(place, volume, mid_near, mid_wrap, weights)
    mid_near, mid_wrap, *early = lax.optimization_barrier((mid_near, mid_wrap, *early))
    pair_near = lax.ppermute(mid_near, x_axes, pair_perm)
    pair_wrap = lax.ppermute(mid_wrap, x_axes, pair_perm)
    pieces = (far, far_near, far_wrap, pair, pair_near, pair_wrap)
    stats, peaks = late_call(place, weights, pieces, early)
    return score_call(stats, all_peaks(peaks))


def solution(mesh):
    fine = jax.sharding.Mesh(
        mesh.devices.reshape(4, 2, 4, 2, 4), ("zh", "core", "x", "zl", "y")
    )
    spec = P(x_axes, y_axes, None)
    return jax.shard_map(
        per_device, mesh=fine, in_specs=(spec,), out_specs=spec, check_vma=False
    )
```

```python
import jax
import jax.numpy as jnp
import ml_dtypes
import numpy as np
from jax import lax
from jax.experimental import pallas as pl
from jax.experimental.pallas import tpu as pltpu
from jax.sharding import PartitionSpec as P

scale_list = (8.0, 4.0, 2.0, 1.0)
radius_list = (24, 12, 6, 3)
x_axes = ("zh", "core")
y_axes = ("x", "zl", "y")
rim = 24
tile_x, tile_y, depth = 24, 32, 128
wide_y = tile_y + 2 * rim
near = (24, 12, 12, 4)
planes = (80, 48, 48, 32)
rows = tile_x * tile_y
z_rows = 192
pitch = 104
mib = 1024 * 1024
log2_e = float(np.log2(np.e))


def taps(scale, radius):
    t = np.arange(-radius, radius + 1).astype(np.float64)
    bell = np.exp(-t * t / (2.0 * scale * scale))
    w0 = bell / bell.sum()
    w1 = -t / (scale * scale) * w0
    w2 = (t * t / scale**4 - 1.0 / (scale * scale)) * w0
    return w0, w1, w2


def band(weights, radius, out_places, in_places):
    lag = out_places[:, None] - in_places[None, :]
    return np.where(np.abs(lag) <= radius, weights[np.clip(lag + radius, 0, 2 * radius)], 0.0)


def split(matrix):
    hi = matrix.astype(np.float32).astype(ml_dtypes.bfloat16)
    lo = (matrix - hi.astype(np.float64)).astype(np.float32).astype(ml_dtypes.bfloat16)
    return hi, lo


def x_places(core, level):
    n = near[level]
    after, before = 2 * rim + np.arange(n), rim - n + np.arange(n)
    sides = [before, after] if core else [after, before]
    padding = np.full(planes[level] - rim - 2 * n, 1000)
    return np.concatenate([rim + np.arange(tile_x)] + sides + [padding])


def constants():
    y_parts, z_parts = [], []
    x_all = np.zeros((2, 4, 3 * tile_x, 2 * depth), ml_dtypes.bfloat16)
    y_places = np.arange(wide_y)
    for level, (scale, radius) in enumerate(zip(scale_list, radius_list)):
        w = taps(scale, radius)
        y_parts += [band(v, radius, rim + np.arange(tile_y), y_places) for v in w]
        for core in range(2):
            places = x_places(core, level)
            hi, lo = split(
                np.concatenate([band(v, radius, rim + np.arange(tile_x), places) for v in w])
            )
            x_all[core, level, :, : 3 * len(places)] = np.concatenate([hi, hi, lo], axis=1)
        for v in w:
            hi, lo = split(band(v * scale * scale, radius, np.arange(depth), np.arange(depth)).T)
            z_parts.append(
                np.concatenate(
                    [np.concatenate([hi, lo], axis=1), np.concatenate([hi, 0 * lo], axis=1)]
                )
            )
    hi, lo = split(np.concatenate(y_parts))
    y_all = np.concatenate([hi, hi, lo, np.zeros((hi.shape[0], 16), hi.dtype)], axis=1)
    return y_all, x_all, np.stack(z_parts)


def halves(value):
    hi = value.astype(jnp.bfloat16)
    lo = (value - hi.astype(jnp.float32)).astype(jnp.bfloat16)
    return hi, lo


def dot(a, b):
    return jnp.dot(a, b, preferred_element_type=jnp.float32)


def y_step(fields, wy, parts, slots):
    both = jnp.concatenate(parts, axis=1)
    both = jnp.concatenate([both[0], both[1]], axis=1)
    hi, lo = halves(both)
    zeros = jnp.zeros((16, 2 * depth), jnp.bfloat16)
    out = dot(wy[0 : 96 * len(slots), :], jnp.concatenate([hi, lo, hi, zeros], axis=0))
    for level, slot in enumerate(slots):
        for k in range(2):
            at = pl.multiple_of((slot + k) * pitch, 8)
            block = out[96 * level : 96 * level + 96, depth * k : depth * (k + 1)]
            fields[level][pl.ds(at, 96), :] = block


def side_steps(fields, wy, parts, before, base):
    for start, stop, levels in ((0, 2, 4), (2, 6, 3), (6, 10, 1), (10, 12, 1)):

        def body(j, carry, levels=levels):
            plane = 2 * (j + before * (11 - 2 * j))
            slots = [base[v] + plane - (rim - near[v]) * before for v in range(levels)]
            y_step(fields, wy, parts(plane), slots)
            return carry

        lax.fori_loop(start, stop, body, 0, unroll=min(4, stop - start))


def by_parity(odd_ref, step, near_rim, wrap_rim):
    for odd, rims in ((0, (wrap_rim, near_rim)), (1, (near_rim, wrap_rim))):

        @pl.when(odd_ref[0] == odd)
        def _(rims=rims):
            step(*rims)


def early_kernel(odd_ref, mid, wy, wx, wz, mid_near, mid_wrap, g8, g4, g2, g1):
    def step(low, high):
        def body(i, carry):
            at = pl.ds(2 * i, 2)
            y_step((g8, g4, g2, g1), wy, [low[at], mid[at], high[at]], [2 * i] * 4)
            return carry

        lax.fori_loop(0, tile_x // 2, body, 0, unroll=4)

    by_parity(odd_ref, step, mid_near, mid_wrap)


def late_kernel(
    core_ref, odd_ref, wy, wx, wz, far, far_near, far_wrap, pair, pair_near, pair_wrap, g8, g4, g2, g1,
    stats, peaks, f8, f4, f2, f1, mixed,
):
    own_fields, fields = (g8, g4, g2, g1), (f8, f4, f2, f1)
    core = core_ref[0]
    f8[pl.ds(2 * rim * pitch, 8 * pitch), :] = jnp.zeros((8 * pitch, depth), jnp.float32)

    def side(tile, before, base):
        def step(low, high):
            def parts(plane):
                at = pl.ds(plane, 2)
                return [low[at], tile[at], high[at]]

            side_steps(fields, wy, parts, before, base)

        return step

    by_parity(odd_ref, side(pair, core, [0] * 4), pair_near, pair_wrap)
    by_parity(odd_ref, side(far, 1 - core, near), far_near, far_wrap)

    lane = lax.broadcasted_iota(jnp.int32, (1, depth), 1)
    peak_row = jnp.zeros((1, depth), jnp.float32)
    for level in range(4):
        own, field = own_fields[level], fields[level]
        count = planes[level]

        def x_body(yp, carry, own=own, field=field, level=level, count=count):
            at = pl.ds(pl.multiple_of(48 * yp, 48), 48)
            for f, first, outs in ((0, 0, 3), (1, 3, 2), (2, 5, 1)):
                pieces = [
                    [
                        own[pl.ds(32 * f + 2 * yp + k, tile_x, stride=pitch), :],
                        field[pl.ds(32 * f + 2 * yp + k, count - tile_x, stride=pitch), :],
                    ]
                    for k in range(2)
                ]
                pieces = [jnp.concatenate(piece, axis=0) for piece in pieces]
                hi, lo = halves(jnp.concatenate(pieces, axis=1))
                data = jnp.concatenate([hi, lo, hi], axis=0)
                out = dot(wx[core, level, 0 : 24 * outs, 0 : 3 * count], data)
                for k in range(outs):
                    u = out[24 * k : 24 * k + 24]
                    u = jnp.concatenate([u[:, :depth], u[:, depth:]], axis=0)
                    hi, lo = halves(u)
                    mixed[first + k, at, 0:depth] = hi
                    mixed[first + k, at, depth : 2 * depth] = lo
            return carry

        lax.fori_loop(0, tile_y // 2, x_body, 0, unroll=16)

        def z_body(c, best, level=level):
            at = pl.ds(pl.multiple_of(c * z_rows, z_rows), z_rows)

            def z_pass(order, chosen):
                data = jnp.concatenate([mixed[p, at, :] for p in chosen], axis=0)
                out = dot(data, wz[3 * level + order])
                out = out[:, :depth] + out[:, depth:]
                return [out[z_rows * k : z_rows * (k + 1)] for k in range(len(chosen))]

            (zz,) = z_pass(2, (0,))
            yz, xz = z_pass(1, (3, 1))
            yy, xy, xx = z_pass(0, (5, 4, 2))
            sq = xy * xy + xz * xz + yz * yz
            stats[3 * level, at, :] = xx + yy + zz
            stats[3 * level + 1, at, :] = xx * yy + (xx + yy) * zz - sq
            energy = xx * xx + yy * yy + zz * zz + 2.0 * sq
            stats[3 * level + 2, at, :] = energy
            return jnp.maximum(best, jnp.max(energy.reshape(z_rows // 8, 8, depth), axis=0))

        best = lax.fori_loop(0, rows // z_rows, z_body, jnp.zeros((8, depth), jnp.float32), unroll=4)
        peak_row = jnp.where(lane == level, jnp.max(best), peak_row)
    peaks[...] = peak_row


def score_kernel(stats, all_peaks, throat, flat):
    peaks = jnp.max(all_peaks[...], axis=0, keepdims=True)
    spreads = [0.25 * peaks[:, level : level + 1] + 1e-06 for level in range(4)]

    def body(c, carry):
        at = pl.ds(pl.multiple_of(c * 24, 24), 24)
        best = None
        for level, spread in enumerate(spreads):
            trace_sum = stats[3 * level, at, :]
            minors = stats[3 * level + 1, at, :]
            energy = stats[3 * level + 2, at, :]
            guard = energy + 0.1 * spread
            root = lax.rsqrt(guard)
            ratio = minors * root * root
            score = (
                (1.0 - jnp.exp2(energy * (-0.5 * log2_e / spread)))
                * jnp.exp2(ratio * ratio * (-2.0 * log2_e))
                * (1.0 - jnp.tanh(2.0 * trace_sum * root))
            )
            best = score if best is None else jnp.maximum(best, score)
        flat[at, :] = 0.5 * best
        return carry

    lax.fori_loop(0, rows // 24, body, 0, unroll=4)
    for i in range(tile_x):
        throat[i] = flat[pl.ds(i, tile_y, stride=tile_x), :]


def vmem(n):
    return [pl.BlockSpec(memory_space=pltpu.VMEM)] * n


def early_call(odd, volume, mid_near, mid_wrap, weights, interpret=False):
    return pl.pallas_call(
        early_kernel,
        out_shape=[jax.ShapeDtypeStruct((tile_x * pitch, depth), jnp.float32)] * 4,
        in_specs=[pl.BlockSpec(memory_space=pltpu.SMEM)] + vmem(6),
        out_specs=vmem(4),
        compiler_params=pltpu.CompilerParams(vmem_limit_bytes=16 * mib),
        interpret=interpret,
    )(odd, volume, *weights, mid_near, mid_wrap)


def late_call(core, odd, weights, pieces, early, interpret=False):
    return pl.pallas_call(
        late_kernel,
        out_shape=(
            jax.ShapeDtypeStruct((12, rows, depth), jnp.float32),
            jax.ShapeDtypeStruct((1, depth), jnp.float32),
        ),
        in_specs=[pl.BlockSpec(memory_space=pltpu.SMEM)] * 2 + vmem(13),
        out_specs=tuple(vmem(2)),
        scratch_shapes=[
            pltpu.VMEM(((count - tile_x) * pitch, depth), jnp.float32) for count in planes
        ]
        + [pltpu.VMEM((6, rows, 2 * depth), jnp.bfloat16)],
        compiler_params=pltpu.CompilerParams(vmem_limit_bytes=24 * mib),
        interpret=interpret,
    )(core, odd, *weights, *pieces, *early)


def score_call(stats, peaks, interpret=False):
    return pl.pallas_call(
        score_kernel,
        out_shape=jax.ShapeDtypeStruct((tile_x, tile_y, depth), jnp.float32),
        in_specs=vmem(2),
        out_specs=vmem(1)[0],
        scratch_shapes=[pltpu.VMEM((rows, depth), jnp.float32)],
        compiler_params=pltpu.CompilerParams(vmem_limit_bytes=8 * mib),
        interpret=interpret,
    )(stats, peaks)


def all_peaks(row):
    axes = x_axes + y_axes
    peers = lax.axis_size(axes)
    spread = jnp.broadcast_to(row[None], (peers, 1, depth))
    return lax.all_to_all(spread, axes, 0, 0, tiled=True).reshape(peers, depth)


def per_device(volume):
    n_x, n_y = lax.axis_size(x_axes), lax.axis_size(y_axes)
    pair_perm = [(i, i ^ 1) for i in range(n_x)]
    far_perm = [(i, i + 1) for i in range(1, n_x - 1, 2)]
    far_perm += [(j, i) for i, j in far_perm]
    near_perm = [(i, i ^ 1) for i in range(n_y)]
    wrap_perm = [(i, i + 1) for i in range(1, n_y - 1, 2)]
    wrap_perm += [(j, i) for i, j in wrap_perm]

    odd = lax.axis_index("y") & 1
    core = lax.axis_index("core")
    volume, core, odd, is_odd, is_even = lax.optimization_barrier(
        (volume, core.reshape(1), odd.reshape(1), odd == 1, odd == 0)
    )

    def edge(tile, top):
        return jnp.where(top, tile[:, tile_y - rim :], tile[:, :rim])

    far = lax.ppermute(volume, x_axes, far_perm)
    mid_wrap = lax.ppermute(edge(volume, is_odd), y_axes, wrap_perm)
    mid_near = lax.ppermute(edge(volume, is_even), y_axes, near_perm)
    pair = lax.ppermute(volume, x_axes, pair_perm)
    far_wrap, far_near = edge(far, is_odd), edge(far, is_even)
    _, _, mid_wrap, mid_near = lax.optimization_barrier((far_wrap, far_near, mid_wrap, mid_near))
    far_wrap = lax.ppermute(far_wrap, y_axes, wrap_perm)
    far_near = lax.ppermute(far_near, y_axes, near_perm)
    weights = [jnp.asarray(w) for w in constants()]
    early = early_call(odd, volume, mid_near, mid_wrap, weights)
    pair_near = lax.ppermute(mid_near, x_axes, pair_perm)
    pair_wrap = lax.ppermute(mid_wrap, x_axes, pair_perm)
    pieces = (far, far_near, far_wrap, pair, pair_near, pair_wrap)
    stats, peaks = late_call(core, odd, weights, pieces, early)
    return score_call(stats, all_peaks(peaks))


def solution(mesh):
    fine = jax.sharding.Mesh(
        mesh.devices.reshape(4, 2, 4, 2, 4), ("zh", "core", "x", "zl", "y")
    )
    spec = P(x_axes, y_axes, None)
    return jax.shard_map(
        per_device, mesh=fine, in_specs=(spec,), out_specs=spec, check_vma=False
    )
```

```python
import jax
import jax.numpy as jnp
import ml_dtypes
import numpy as np
from jax import lax
from jax.experimental import pallas as pl
from jax.experimental.pallas import tpu as pltpu
from jax.sharding import PartitionSpec as P

scale_list = (8.0, 4.0, 2.0, 1.0)
radius_list = (24, 12, 6, 3)
x_axes = ("zh", "core")
y_axes = ("x", "zl", "y")
rim = 24
tile_x, tile_y, depth = 24, 32, 128
wide_y = tile_y + 2 * rim
near = (24, 12, 12, 4)
planes = (80, 48, 48, 32)
rows = tile_x * tile_y
z_rows = 192
pitch = 104
mib = 1024 * 1024
log2_e = float(np.log2(np.e))


def taps(scale, radius):
    t = np.arange(-radius, radius + 1).astype(np.float64)
    bell = np.exp(-t * t / (2.0 * scale * scale))
    w0 = bell / bell.sum()
    w1 = -t / (scale * scale) * w0
    w2 = (t * t / scale**4 - 1.0 / (scale * scale)) * w0
    return w0, w1, w2


def band(weights, radius, out_places, in_places):
    lag = out_places[:, None] - in_places[None, :]
    return np.where(np.abs(lag) <= radius, weights[np.clip(lag + radius, 0, 2 * radius)], 0.0)


def split(matrix):
    hi = matrix.astype(np.float32).astype(ml_dtypes.bfloat16)
    lo = (matrix - hi.astype(np.float64)).astype(np.float32).astype(ml_dtypes.bfloat16)
    return hi, lo


def x_places(core, level):
    n = near[level]
    after, before = 2 * rim + np.arange(n), rim - n + np.arange(n)
    sides = [before, after] if core else [after, before]
    padding = np.full(planes[level] - rim - 2 * n, 1000)
    return np.concatenate([rim + np.arange(tile_x)] + sides + [padding])


def constants():
    y_parts, z_parts = [], []
    x_all = np.zeros((2, 4, 3 * tile_x, 2 * depth), ml_dtypes.bfloat16)
    y_places = np.arange(wide_y)
    for level, (scale, radius) in enumerate(zip(scale_list, radius_list)):
        w = taps(scale, radius)
        y_parts += [band(v, radius, rim + np.arange(tile_y), y_places) for v in w]
        for core in range(2):
            places = x_places(core, level)
            hi, lo = split(
                np.concatenate([band(v, radius, rim + np.arange(tile_x), places) for v in w])
            )
            x_all[core, level, :, : 3 * len(places)] = np.concatenate([hi, hi, lo], axis=1)
        for v in w:
            hi, lo = split(band(v * scale * scale, radius, np.arange(depth), np.arange(depth)).T)
            z_parts.append(
                np.concatenate(
                    [np.concatenate([hi, lo], axis=1), np.concatenate([hi, 0 * lo], axis=1)]
                )
            )
    hi, lo = split(np.concatenate(y_parts))
    y_all = np.concatenate([hi, hi, lo, np.zeros((hi.shape[0], 16), hi.dtype)], axis=1)
    return y_all, x_all, np.stack(z_parts)


def halves(value):
    hi = value.astype(jnp.bfloat16)
    lo = (value - hi.astype(jnp.float32)).astype(jnp.bfloat16)
    return hi, lo


def dot(a, b):
    return jnp.dot(a, b, preferred_element_type=jnp.float32)


def y_step(fields, wy, parts, slots):
    both = jnp.concatenate(parts, axis=1)
    both = jnp.concatenate([both[0], both[1]], axis=1)
    hi, lo = halves(both)
    zeros = jnp.zeros((16, 2 * depth), jnp.bfloat16)
    out = dot(wy[0 : 96 * len(slots), :], jnp.concatenate([hi, lo, hi, zeros], axis=0))
    for level, slot in enumerate(slots):
        for k in range(2):
            at = pl.multiple_of((slot + k) * pitch, 8)
            block = out[96 * level : 96 * level + 96, depth * k : depth * (k + 1)]
            fields[level][pl.ds(at, 96), :] = block


def side_steps(fields, wy, parts, before, base):
    for start, stop, levels in ((0, 2, 4), (2, 6, 3), (6, 12, 1)):

        def body(j, carry, levels=levels):
            plane = 2 * (j + before * (11 - 2 * j))
            slots = [base[v] + plane - (rim - near[v]) * before for v in range(levels)]
            y_step(fields, wy, parts(plane), slots)
            return carry

        lax.fori_loop(start, stop, body, 0, unroll=stop - start)


def by_parity(odd_ref, step, near_rim, wrap_rim):
    for odd, rims in ((0, (wrap_rim, near_rim)), (1, (near_rim, wrap_rim))):

        @pl.when(odd_ref[0] == odd)
        def _(rims=rims):
            step(*rims)


def early_kernel(odd_ref, mid, wy, wx, wz, mid_near, mid_wrap, g8, g4, g2, g1):
    def step(low, high):
        def body(i, carry):
            at = pl.ds(2 * i, 2)
            y_step((g8, g4, g2, g1), wy, [low[at], mid[at], high[at]], [2 * i] * 4)
            return carry

        lax.fori_loop(0, tile_x // 2, body, 0, unroll=12)

    by_parity(odd_ref, step, mid_near, mid_wrap)


def late_kernel(
    core_ref, odd_ref, wy, wx, wz, far, far_near, far_wrap, pair, pair_near, pair_wrap, g8, g4, g2, g1,
    stats, peaks, f8, f4, f2, f1, mixed,
):
    own_fields, fields = (g8, g4, g2, g1), (f8, f4, f2, f1)
    core = core_ref[0]
    f8[pl.ds(2 * rim * pitch, 8 * pitch), :] = jnp.zeros((8 * pitch, depth), jnp.float32)

    def side(tile, before, base):
        def step(low, high):
            def parts(plane):
                at = pl.ds(plane, 2)
                return [low[at], tile[at], high[at]]

            side_steps(fields, wy, parts, before, base)

        return step

    by_parity(odd_ref, side(pair, core, [0] * 4), pair_near, pair_wrap)
    by_parity(odd_ref, side(far, 1 - core, near), far_near, far_wrap)

    def x_step(level, yp):
        own, field, count = own_fields[level], fields[level], planes[level]
        at = pl.ds(48 * yp, 48)
        for f, first, outs in ((0, 0, 3), (1, 3, 2), (2, 5, 1)):
            pieces = [
                [
                    own[pl.ds(32 * f + 2 * yp + k, tile_x, stride=pitch), :],
                    field[pl.ds(32 * f + 2 * yp + k, count - tile_x, stride=pitch), :],
                ]
                for k in range(2)
            ]
            pieces = [jnp.concatenate(piece, axis=0) for piece in pieces]
            hi, lo = halves(jnp.concatenate(pieces, axis=1))
            data = jnp.concatenate([hi, lo, hi], axis=0)
            out = dot(wx[core, level, 0 : 24 * outs, 0 : 3 * count], data)
            for k in range(outs):
                u = out[24 * k : 24 * k + 24]
                u = jnp.concatenate([u[:, :depth], u[:, depth:]], axis=0)
                hi, lo = halves(u)
                mixed[level, first + k, at, 0:depth] = hi
                mixed[level, first + k, at, depth : 2 * depth] = lo

    def z_step(level, c, best):
        at = pl.ds(c * z_rows, z_rows)

        def z_pass(order, chosen):
            data = jnp.concatenate([mixed[level, p, at, :] for p in chosen], axis=0)
            out = dot(data, wz[3 * level + order])
            out = out[:, :depth] + out[:, depth:]
            return [out[z_rows * k : z_rows * (k + 1)] for k in range(len(chosen))]

        (zz,) = z_pass(2, (0,))
        yz, xz = z_pass(1, (3, 1))
        yy, xy, xx = z_pass(0, (5, 4, 2))
        sq = xy * xy + xz * xz + yz * yz
        stats[3 * level, at, :] = xx + yy + zz
        stats[3 * level + 1, at, :] = xx * yy + (xx + yy) * zz - sq
        energy = xx * xx + yy * yy + zz * zz + 2.0 * sq
        stats[3 * level + 2, at, :] = energy
        return jnp.maximum(best, jnp.max(energy.reshape(z_rows // 8, 8, depth), axis=0))

    lane = lax.broadcasted_iota(jnp.int32, (1, depth), 1)
    peak_row = jnp.zeros((1, depth), jnp.float32)
    blocks = rows // z_rows
    steps = tile_y // 2 // blocks
    for level in range(5):
        best = jnp.zeros((8, depth), jnp.float32)
        for c in range(blocks):
            if level < 4:
                for yp in range(steps * c, steps * (c + 1)):
                    x_step(level, yp)
            if level > 0:
                best = z_step(level - 1, c, best)
        if level > 0:
            peak_row = jnp.where(lane == level - 1, jnp.max(best), peak_row)
    peaks[...] = peak_row


def score_kernel(stats, all_peaks, throat, flat):
    peaks = jnp.max(all_peaks[...], axis=0, keepdims=True)
    spreads = [0.25 * peaks[:, level : level + 1] + 1e-06 for level in range(4)]

    def body(c, carry):
        at = pl.ds(pl.multiple_of(c * 24, 24), 24)
        best = None
        for level, spread in enumerate(spreads):
            trace_sum = stats[3 * level, at, :]
            minors = stats[3 * level + 1, at, :]
            energy = stats[3 * level + 2, at, :]
            guard = energy + 0.1 * spread
            root = lax.rsqrt(guard)
            ratio = minors * root * root
            score = (
                (1.0 - jnp.exp2(energy * (-0.5 * log2_e / spread)))
                * jnp.exp2(ratio * ratio * (-2.0 * log2_e))
                * (1.0 - jnp.tanh(2.0 * trace_sum * root))
            )
            best = score if best is None else jnp.maximum(best, score)
        flat[at, :] = 0.5 * best
        return carry

    lax.fori_loop(0, rows // 24, body, 0, unroll=32)
    for i in range(tile_x):
        throat[i] = flat[pl.ds(i, tile_y, stride=tile_x), :]


def vmem(n):
    return [pl.BlockSpec(memory_space=pltpu.VMEM)] * n


def early_call(odd, volume, mid_near, mid_wrap, weights, interpret=False):
    return pl.pallas_call(
        early_kernel,
        out_shape=[jax.ShapeDtypeStruct((tile_x * pitch, depth), jnp.float32)] * 4,
        in_specs=[pl.BlockSpec(memory_space=pltpu.SMEM)] + vmem(6),
        out_specs=vmem(4),
        compiler_params=pltpu.CompilerParams(vmem_limit_bytes=16 * mib),
        interpret=interpret,
    )(odd, volume, *weights, mid_near, mid_wrap)


def late_call(core, odd, weights, pieces, early, interpret=False):
    return pl.pallas_call(
        late_kernel,
        out_shape=(
            jax.ShapeDtypeStruct((12, rows, depth), jnp.float32),
            jax.ShapeDtypeStruct((1, depth), jnp.float32),
        ),
        in_specs=[pl.BlockSpec(memory_space=pltpu.SMEM)] * 2 + vmem(13),
        out_specs=tuple(vmem(2)),
        scratch_shapes=[
            pltpu.VMEM(((count - tile_x) * pitch, depth), jnp.float32) for count in planes
        ]
        + [pltpu.VMEM((4, 6, rows, 2 * depth), jnp.bfloat16)],
        compiler_params=pltpu.CompilerParams(vmem_limit_bytes=28 * mib),
        interpret=interpret,
    )(core, odd, *weights, *pieces, *early)


def score_call(stats, peaks, interpret=False):
    return pl.pallas_call(
        score_kernel,
        out_shape=jax.ShapeDtypeStruct((tile_x, tile_y, depth), jnp.float32),
        in_specs=vmem(2),
        out_specs=vmem(1)[0],
        scratch_shapes=[pltpu.VMEM((rows, depth), jnp.float32)],
        compiler_params=pltpu.CompilerParams(vmem_limit_bytes=8 * mib),
        interpret=interpret,
    )(stats, peaks)


def all_peaks(row):
    axes = x_axes + y_axes
    peers = lax.axis_size(axes)
    spread = jnp.broadcast_to(row[None], (peers, 1, depth))
    return lax.all_to_all(spread, axes, 0, 0, tiled=True).reshape(peers, depth)


def per_device(volume):
    n_x, n_y = lax.axis_size(x_axes), lax.axis_size(y_axes)
    pair_perm = [(i, i ^ 1) for i in range(n_x)]
    far_perm = [(i, i + 1) for i in range(1, n_x - 1, 2)]
    far_perm += [(j, i) for i, j in far_perm]
    near_perm = [(i, i ^ 1) for i in range(n_y)]
    wrap_perm = [(i, i + 1) for i in range(1, n_y - 1, 2)]
    wrap_perm += [(j, i) for i, j in wrap_perm]

    odd = lax.axis_index("y") & 1
    core = lax.axis_index("core")
    volume, core, odd, is_odd, is_even = lax.optimization_barrier(
        (volume, core.reshape(1), odd.reshape(1), odd == 1, odd == 0)
    )

    def edge(tile, top):
        return jnp.where(top, tile[:, tile_y - rim :], tile[:, :rim])

    far = lax.ppermute(volume, x_axes, far_perm)
    mid_wrap = lax.ppermute(edge(volume, is_odd), y_axes, wrap_perm)
    mid_near = lax.ppermute(edge(volume, is_even), y_axes, near_perm)
    pair = lax.ppermute(volume, x_axes, pair_perm)
    far_wrap, far_near = edge(far, is_odd), edge(far, is_even)
    _, _, mid_wrap, mid_near = lax.optimization_barrier((far_wrap, far_near, mid_wrap, mid_near))
    far_wrap = lax.ppermute(far_wrap, y_axes, wrap_perm)
    far_near = lax.ppermute(far_near, y_axes, near_perm)
    weights = [jnp.asarray(w) for w in constants()]
    early = early_call(odd, volume, mid_near, mid_wrap, weights)
    pair_near = lax.ppermute(mid_near, x_axes, pair_perm)
    pair_wrap = lax.ppermute(mid_wrap, x_axes, pair_perm)
    pieces = (far, far_near, far_wrap, pair, pair_near, pair_wrap)
    stats, peaks = late_call(core, odd, weights, pieces, early)
    return score_call(stats, all_peaks(peaks))


def solution(mesh):
    fine = jax.sharding.Mesh(
        mesh.devices.reshape(4, 2, 4, 2, 4), ("zh", "core", "x", "zl", "y")
    )
    spec = P(x_axes, y_axes, None)
    return jax.shard_map(
        per_device, mesh=fine, in_specs=(spec,), out_specs=spec, check_vma=False
    )
```

```python
import jax
import jax.numpy as jnp
import ml_dtypes
import numpy as np
from jax import lax
from jax.experimental import pallas as pl
from jax.experimental.pallas import tpu as pltpu
from jax.sharding import PartitionSpec as P

scale_list = (8.0, 4.0, 2.0, 1.0)
radius_list = (24, 12, 6, 3)
x_axes = ("zh", "core")
y_axes = ("x", "zl", "y")
rim = 24
tile_x, tile_y, depth = 24, 32, 128
wide_y = tile_y + 2 * rim
near = (24, 12, 12, 4)
planes = (80, 48, 48, 32)
rows = tile_x * tile_y
z_rows = 96
pitch = 104
mib = 1024 * 1024
log2_e = float(np.log2(np.e))


def taps(scale, radius):
    t = np.arange(-radius, radius + 1).astype(np.float64)
    bell = np.exp(-t * t / (2.0 * scale * scale))
    w0 = bell / bell.sum()
    w1 = -t / (scale * scale) * w0
    w2 = (t * t / scale**4 - 1.0 / (scale * scale)) * w0
    return w0, w1, w2


def band(weights, radius, out_places, in_places):
    lag = out_places[:, None] - in_places[None, :]
    return np.where(np.abs(lag) <= radius, weights[np.clip(lag + radius, 0, 2 * radius)], 0.0)


def split(matrix):
    hi = matrix.astype(np.float32).astype(ml_dtypes.bfloat16)
    lo = (matrix - hi.astype(np.float64)).astype(np.float32).astype(ml_dtypes.bfloat16)
    return hi, lo


def x_places(core, level):
    n = near[level]
    after, before = 2 * rim + np.arange(n), rim - n + np.arange(n)
    sides = [before, after] if core else [after, before]
    padding = np.full(planes[level] - rim - 2 * n, 1000)
    return np.concatenate([rim + np.arange(tile_x)] + sides + [padding])


def constants():
    y_parts, z_parts = [], []
    x_all = np.zeros((2, 4, 3 * tile_x, 2 * depth), ml_dtypes.bfloat16)
    y_places = np.arange(wide_y)
    for level, (scale, radius) in enumerate(zip(scale_list, radius_list)):
        w = taps(scale, radius)
        y_parts += [band(v, radius, rim + np.arange(tile_y), y_places) for v in w]
        for core in range(2):
            places = x_places(core, level)
            hi, lo = split(
                np.concatenate([band(v, radius, rim + np.arange(tile_x), places) for v in w])
            )
            x_all[core, level, :, : 3 * len(places)] = np.concatenate([hi, hi, lo], axis=1)
        for v in w:
            hi, lo = split(band(v * scale * scale, radius, np.arange(depth), np.arange(depth)).T)
            z_parts.append(
                np.concatenate(
                    [np.concatenate([hi, lo], axis=1), np.concatenate([hi, 0 * lo], axis=1)]
                )
            )
    hi, lo = split(np.concatenate(y_parts))
    y_all = np.concatenate([hi, hi, lo, np.zeros((hi.shape[0], 16), hi.dtype)], axis=1)
    return y_all, x_all, np.stack(z_parts)


def halves(value):
    hi = value.astype(jnp.bfloat16)
    lo = (value - hi.astype(jnp.float32)).astype(jnp.bfloat16)
    return hi, lo


def dot(a, b):
    return jnp.dot(a, b, preferred_element_type=jnp.float32)


def y_step(fields, wy, parts, slots):
    both = jnp.concatenate(parts, axis=1)
    both = jnp.concatenate([both[0], both[1]], axis=1)
    hi, lo = halves(both)
    zeros = jnp.zeros((16, 2 * depth), jnp.bfloat16)
    out = dot(wy[0 : 96 * len(slots), :], jnp.concatenate([hi, lo, hi, zeros], axis=0))
    for level, slot in enumerate(slots):
        for k in range(2):
            at = pl.multiple_of((slot + k) * pitch, 8)
            block = out[96 * level : 96 * level + 96, depth * k : depth * (k + 1)]
            fields[level][pl.ds(at, 96), :] = block


def side_steps(fields, wy, parts, before, base):
    for start, stop, levels in ((0, 2, 4), (2, 6, 3), (6, 12, 1)):

        def body(j, carry, levels=levels):
            plane = 2 * (j + before * (11 - 2 * j))
            slots = [base[v] + plane - (rim - near[v]) * before for v in range(levels)]
            y_step(fields, wy, parts(plane), slots)
            return carry

        lax.fori_loop(start, stop, body, 0, unroll=stop - start)


def by_parity(odd_ref, step, near_rim, wrap_rim):
    for odd, rims in ((0, (wrap_rim, near_rim)), (1, (near_rim, wrap_rim))):

        @pl.when(odd_ref[0] == odd)
        def _(rims=rims):
            step(*rims)


def early_kernel(odd_ref, mid, wy, wx, wz, mid_near, mid_wrap, g8, g4, g2, g1):
    def step(low, high):
        def body(i, carry):
            at = pl.ds(2 * i, 2)
            y_step((g8, g4, g2, g1), wy, [low[at], mid[at], high[at]], [2 * i] * 4)
            return carry

        lax.fori_loop(0, tile_x // 2, body, 0, unroll=12)

    by_parity(odd_ref, step, mid_near, mid_wrap)


def late_kernel(
    core_ref, odd_ref, wy, wx, wz, far, far_near, far_wrap, pair, pair_near, pair_wrap, g8, g4, g2, g1,
    stats, peaks, f8, f4, f2, f1, mixed,
):
    own_fields, fields = (g8, g4, g2, g1), (f8, f4, f2, f1)
    core = core_ref[0]
    f8[pl.ds(2 * rim * pitch, 8 * pitch), :] = jnp.zeros((8 * pitch, depth), jnp.float32)

    def side(tile, before, base):
        def step(low, high):
            def parts(plane):
                at = pl.ds(plane, 2)
                return [low[at], tile[at], high[at]]

            side_steps(fields, wy, parts, before, base)

        return step

    by_parity(odd_ref, side(pair, core, [0] * 4), pair_near, pair_wrap)
    by_parity(odd_ref, side(far, 1 - core, near), far_near, far_wrap)

    def x_step(level, yp):
        own, field, count = own_fields[level], fields[level], planes[level]
        at = pl.ds(48 * yp, 48)
        for f, first, outs in ((0, 0, 3), (1, 3, 2), (2, 5, 1)):
            pieces = [
                [
                    own[pl.ds(32 * f + 2 * yp + k, tile_x, stride=pitch), :],
                    field[pl.ds(32 * f + 2 * yp + k, count - tile_x, stride=pitch), :],
                ]
                for k in range(2)
            ]
            pieces = [jnp.concatenate(piece, axis=0) for piece in pieces]
            hi, lo = halves(jnp.concatenate(pieces, axis=1))
            data = jnp.concatenate([hi, lo, hi], axis=0)
            out = dot(wx[core, level, 0 : 24 * outs, 0 : 3 * count], data)
            for k in range(outs):
                u = out[24 * k : 24 * k + 24]
                u = jnp.concatenate([u[:, :depth], u[:, depth:]], axis=0)
                hi, lo = halves(u)
                mixed[level, first + k, at, 0:depth] = hi
                mixed[level, first + k, at, depth : 2 * depth] = lo

    def z_step(level, c, best):
        at = pl.ds(c * z_rows, z_rows)

        def z_pass(order, chosen):
            data = jnp.concatenate([mixed[level, p, at, :] for p in chosen], axis=0)
            out = dot(data, wz[3 * level + order])
            out = out[:, :depth] + out[:, depth:]
            return [out[z_rows * k : z_rows * (k + 1)] for k in range(len(chosen))]

        (zz,) = z_pass(2, (0,))
        yz, xz = z_pass(1, (3, 1))
        yy, xy, xx = z_pass(0, (5, 4, 2))
        sq = xy * xy + xz * xz + yz * yz
        stats[3 * level, at, :] = xx + yy + zz
        stats[3 * level + 1, at, :] = xx * yy + (xx + yy) * zz - sq
        energy = xx * xx + yy * yy + zz * zz + 2.0 * sq
        stats[3 * level + 2, at, :] = energy
        return jnp.maximum(best, jnp.max(energy.reshape(z_rows // 8, 8, depth), axis=0))

    lane = lax.broadcasted_iota(jnp.int32, (1, depth), 1)
    peak_row = jnp.zeros((1, depth), jnp.float32)
    blocks = rows // z_rows
    steps = tile_y // 2 // blocks
    for level in range(5):
        best = jnp.zeros((8, depth), jnp.float32)
        for c in range(blocks):
            if level < 4:
                for yp in range(steps * c, steps * (c + 1)):
                    x_step(level, yp)
            if level > 0:
                best = z_step(level - 1, c, best)
        if level > 0:
            peak_row = jnp.where(lane == level - 1, jnp.max(best), peak_row)
    peaks[...] = peak_row


def score_kernel(stats, all_peaks, throat, flat):
    peaks = jnp.max(all_peaks[...], axis=0, keepdims=True)
    spreads = [0.25 * peaks[:, level : level + 1] + 1e-06 for level in range(4)]

    def body(c, carry):
        at = pl.ds(pl.multiple_of(c * 24, 24), 24)
        best = None
        for level, spread in enumerate(spreads):
            trace_sum = stats[3 * level, at, :]
            minors = stats[3 * level + 1, at, :]
            energy = stats[3 * level + 2, at, :]
            guard = energy + 0.1 * spread
            root = lax.rsqrt(guard)
            ratio = minors * root * root
            score = (
                (1.0 - jnp.exp2(energy * (-0.5 * log2_e / spread)))
                * jnp.exp2(ratio * ratio * (-2.0 * log2_e))
                * (1.0 - jnp.tanh(2.0 * trace_sum * root))
            )
            best = score if best is None else jnp.maximum(best, score)
        flat[at, :] = 0.5 * best
        return carry

    lax.fori_loop(0, rows // 24, body, 0, unroll=32)
    for i in range(tile_x):
        throat[i] = flat[pl.ds(i, tile_y, stride=tile_x), :]


def vmem(n):
    return [pl.BlockSpec(memory_space=pltpu.VMEM)] * n


def early_call(odd, volume, mid_near, mid_wrap, weights, interpret=False):
    return pl.pallas_call(
        early_kernel,
        out_shape=[jax.ShapeDtypeStruct((tile_x * pitch, depth), jnp.float32)] * 4,
        in_specs=[pl.BlockSpec(memory_space=pltpu.SMEM)] + vmem(6),
        out_specs=vmem(4),
        compiler_params=pltpu.CompilerParams(vmem_limit_bytes=16 * mib),
        interpret=interpret,
    )(odd, volume, *weights, mid_near, mid_wrap)


def late_call(core, odd, weights, pieces, early, interpret=False):
    return pl.pallas_call(
        late_kernel,
        out_shape=(
            jax.ShapeDtypeStruct((12, rows, depth), jnp.float32),
            jax.ShapeDtypeStruct((1, depth), jnp.float32),
        ),
        in_specs=[pl.BlockSpec(memory_space=pltpu.SMEM)] * 2 + vmem(13),
        out_specs=tuple(vmem(2)),
        scratch_shapes=[
            pltpu.VMEM(((count - tile_x) * pitch, depth), jnp.float32) for count in planes
        ]
        + [pltpu.VMEM((4, 6, rows, 2 * depth), jnp.bfloat16)],
        compiler_params=pltpu.CompilerParams(vmem_limit_bytes=28 * mib),
        interpret=interpret,
    )(core, odd, *weights, *pieces, *early)


def score_call(stats, peaks, interpret=False):
    return pl.pallas_call(
        score_kernel,
        out_shape=jax.ShapeDtypeStruct((tile_x, tile_y, depth), jnp.float32),
        in_specs=vmem(2),
        out_specs=vmem(1)[0],
        scratch_shapes=[pltpu.VMEM((rows, depth), jnp.float32)],
        compiler_params=pltpu.CompilerParams(vmem_limit_bytes=8 * mib),
        interpret=interpret,
    )(stats, peaks)


def all_peaks(row):
    axes = x_axes + y_axes
    peers = lax.axis_size(axes)
    spread = jnp.broadcast_to(row[None], (peers, 1, depth))
    return lax.all_to_all(spread, axes, 0, 0, tiled=True).reshape(peers, depth)


def per_device(volume):
    n_x, n_y = lax.axis_size(x_axes), lax.axis_size(y_axes)
    pair_perm = [(i, i ^ 1) for i in range(n_x)]
    far_perm = [(i, i + 1) for i in range(1, n_x - 1, 2)]
    far_perm += [(j, i) for i, j in far_perm]
    near_perm = [(i, i ^ 1) for i in range(n_y)]
    wrap_perm = [(i, i + 1) for i in range(1, n_y - 1, 2)]
    wrap_perm += [(j, i) for i, j in wrap_perm]

    odd = lax.axis_index("y") & 1
    core = lax.axis_index("core")
    volume, core, odd, is_odd, is_even = lax.optimization_barrier(
        (volume, core.reshape(1), odd.reshape(1), odd == 1, odd == 0)
    )

    def edge(tile, top):
        return jnp.where(top, tile[:, tile_y - rim :], tile[:, :rim])

    far = lax.ppermute(volume, x_axes, far_perm)
    mid_wrap = lax.ppermute(edge(volume, is_odd), y_axes, wrap_perm)
    mid_near = lax.ppermute(edge(volume, is_even), y_axes, near_perm)
    pair = lax.ppermute(volume, x_axes, pair_perm)
    far_wrap, far_near = edge(far, is_odd), edge(far, is_even)
    _, _, mid_wrap, mid_near = lax.optimization_barrier((far_wrap, far_near, mid_wrap, mid_near))
    far_wrap = lax.ppermute(far_wrap, y_axes, wrap_perm)
    far_near = lax.ppermute(far_near, y_axes, near_perm)
    weights = [jnp.asarray(w) for w in constants()]
    early = early_call(odd, volume, mid_near, mid_wrap, weights)
    pair_near = lax.ppermute(mid_near, x_axes, pair_perm)
    pair_wrap = lax.ppermute(mid_wrap, x_axes, pair_perm)
    pieces = (far, far_near, far_wrap, pair, pair_near, pair_wrap)
    stats, peaks = late_call(core, odd, weights, pieces, early)
    return score_call(stats, all_peaks(peaks))


def solution(mesh):
    fine = jax.sharding.Mesh(
        mesh.devices.reshape(4, 2, 4, 2, 4), ("zh", "core", "x", "zl", "y")
    )
    spec = P(x_axes, y_axes, None)
    return jax.shard_map(
        per_device, mesh=fine, in_specs=(spec,), out_specs=spec, check_vma=False
    )
```

```python
import jax
import jax.numpy as jnp
import ml_dtypes
import numpy as np
from jax import lax
from jax.experimental import pallas as pl
from jax.experimental.pallas import tpu as pltpu
from jax.sharding import PartitionSpec as P

scale_list = (8.0, 4.0, 2.0, 1.0)
radius_list = (24, 12, 6, 3)
x_axes = ("zh", "core")
y_axes = ("x", "zl", "y")
rim = 24
tile_x, tile_y, depth = 24, 32, 128
wide_y = tile_y + 2 * rim
near = (24, 12, 12, 4)
planes = (80, 48, 48, 32)
rows = tile_x * tile_y
z_rows = 192
pitch = 104
mib = 1024 * 1024
log2_e = float(np.log2(np.e))


def taps(scale, radius):
    t = np.arange(-radius, radius + 1).astype(np.float64)
    bell = np.exp(-t * t / (2.0 * scale * scale))
    w0 = bell / bell.sum()
    w1 = -t / (scale * scale) * w0
    w2 = (t * t / scale**4 - 1.0 / (scale * scale)) * w0
    return w0, w1, w2


def band(weights, radius, out_places, in_places):
    lag = out_places[:, None] - in_places[None, :]
    return np.where(np.abs(lag) <= radius, weights[np.clip(lag + radius, 0, 2 * radius)], 0.0)


def split(matrix):
    hi = matrix.astype(np.float32).astype(ml_dtypes.bfloat16)
    lo = (matrix - hi.astype(np.float64)).astype(np.float32).astype(ml_dtypes.bfloat16)
    return hi, lo


def x_places(core, level):
    n = near[level]
    after, before = 2 * rim + np.arange(n), rim - n + np.arange(n)
    sides = [before, after] if core else [after, before]
    padding = np.full(planes[level] - rim - 2 * n, 1000)
    return np.concatenate([rim + np.arange(tile_x)] + sides + [padding])


def constants():
    y_parts, z_parts = [], []
    x_all = np.zeros((2, 4, 3 * tile_x, 2 * depth), ml_dtypes.bfloat16)
    y_places = np.arange(wide_y)
    for level, (scale, radius) in enumerate(zip(scale_list, radius_list)):
        w = taps(scale, radius)
        y_parts += [band(v, radius, rim + np.arange(tile_y), y_places) for v in w]
        for core in range(2):
            places = x_places(core, level)
            hi, lo = split(
                np.concatenate([band(v, radius, rim + np.arange(tile_x), places) for v in w])
            )
            x_all[core, level, :, : 3 * len(places)] = np.concatenate([hi, hi, lo], axis=1)
        for v in w:
            hi, lo = split(band(v * scale * scale, radius, np.arange(depth), np.arange(depth)).T)
            z_parts.append(
                np.concatenate(
                    [np.concatenate([hi, lo], axis=1), np.concatenate([hi, 0 * lo], axis=1)]
                )
            )
    hi, lo = split(np.concatenate(y_parts))
    y_all = np.concatenate([hi, hi, lo, np.zeros((hi.shape[0], 16), hi.dtype)], axis=1)
    return y_all, x_all, np.stack(z_parts)


def halves(value):
    hi = value.astype(jnp.bfloat16)
    lo = (value - hi.astype(jnp.float32)).astype(jnp.bfloat16)
    return hi, lo


def dot(a, b):
    return jnp.dot(a, b, preferred_element_type=jnp.float32)


def y_step(fields, wy, parts, slots):
    both = jnp.concatenate(parts, axis=1)
    both = jnp.concatenate([both[0], both[1]], axis=1)
    hi, lo = halves(both)
    zeros = jnp.zeros((16, 2 * depth), jnp.bfloat16)
    out = dot(wy[0 : 96 * len(slots), :], jnp.concatenate([hi, lo, hi, zeros], axis=0))
    for level, slot in enumerate(slots):
        for k in range(2):
            at = pl.multiple_of((slot + k) * pitch, 8)
            block = out[96 * level : 96 * level + 96, depth * k : depth * (k + 1)]
            fields[level][pl.ds(at, 96), :] = block


def side_steps(fields, wy, parts, before, base):
    for start, stop, levels in ((0, 2, 4), (2, 6, 3), (6, 12, 1)):

        def body(j, carry, levels=levels):
            plane = 2 * (j + before * (11 - 2 * j))
            slots = [base[v] + plane - (rim - near[v]) * before for v in range(levels)]
            y_step(fields, wy, parts(plane), slots)
            return carry

        lax.fori_loop(start, stop, body, 0, unroll=stop - start)


def by_parity(odd_ref, step, near_rim, wrap_rim):
    for odd, rims in ((0, (wrap_rim, near_rim)), (1, (near_rim, wrap_rim))):

        @pl.when(odd_ref[0] == odd)
        def _(rims=rims):
            step(*rims)


def early_kernel(odd_ref, mid, wy, wx, wz, mid_near, mid_wrap, g8, g4, g2, g1):
    def step(low, high):
        def body(i, carry):
            at = pl.ds(2 * i, 2)
            y_step((g8, g4, g2, g1), wy, [low[at], mid[at], high[at]], [2 * i] * 4)
            return carry

        lax.fori_loop(0, tile_x // 2, body, 0, unroll=12)

    by_parity(odd_ref, step, mid_near, mid_wrap)


def late_kernel(
    core_ref, odd_ref, wy, wx, wz, far, far_near, far_wrap, pair, pair_near, pair_wrap, g8, g4, g2, g1,
    stats, peaks, f8, f4, f2, f1, mixed,
):
    own_fields, fields = (g8, g4, g2, g1), (f8, f4, f2, f1)
    core = core_ref[0]
    f8[pl.ds(2 * rim * pitch, 8 * pitch), :] = jnp.zeros((8 * pitch, depth), jnp.float32)

    def side(tile, before, base):
        def step(low, high):
            def parts(plane):
                at = pl.ds(plane, 2)
                return [low[at], tile[at], high[at]]

            side_steps(fields, wy, parts, before, base)

        return step

    by_parity(odd_ref, side(pair, core, [0] * 4), pair_near, pair_wrap)
    by_parity(odd_ref, side(far, 1 - core, near), far_near, far_wrap)

    def x_step(level, yp):
        own, field, count = own_fields[level], fields[level], planes[level]
        at = pl.ds(48 * yp, 48)
        for f, first, outs in ((0, 0, 3), (1, 3, 2), (2, 5, 1)):
            pieces = [
                [
                    own[pl.ds(32 * f + 2 * yp + k, tile_x, stride=pitch), :],
                    field[pl.ds(32 * f + 2 * yp + k, count - tile_x, stride=pitch), :],
                ]
                for k in range(2)
            ]
            pieces = [jnp.concatenate(piece, axis=0) for piece in pieces]
            hi, lo = halves(jnp.concatenate(pieces, axis=1))
            data = jnp.concatenate([hi, lo, hi], axis=0)
            out = dot(wx[core, level, 0 : 24 * outs, 0 : 3 * count], data)
            for k in range(outs):
                u = out[24 * k : 24 * k + 24]
                u = jnp.concatenate([u[:, :depth], u[:, depth:]], axis=0)
                hi, lo = halves(u)
                mixed[level, first + k, at, 0:depth] = hi
                mixed[level, first + k, at, depth : 2 * depth] = lo

    def z_step(level, c, best):
        at = pl.ds(c * z_rows, z_rows)

        def z_pass(order, chosen):
            data = jnp.concatenate([mixed[level, p, at, :] for p in chosen], axis=0)
            out = dot(data, wz[3 * level + order])
            out = out[:, :depth] + out[:, depth:]
            return [out[z_rows * k : z_rows * (k + 1)] for k in range(len(chosen))]

        (zz,) = z_pass(2, (0,))
        yz, xz = z_pass(1, (3, 1))
        yy, xy, xx = z_pass(0, (5, 4, 2))
        sq = xy * xy + xz * xz + yz * yz
        stats[3 * level, at, :] = xx + yy + zz
        stats[3 * level + 1, at, :] = xx * yy + (xx + yy) * zz - sq
        energy = xx * xx + yy * yy + zz * zz + 2.0 * sq
        stats[3 * level + 2, at, :] = energy
        return jnp.maximum(best, jnp.max(energy.reshape(z_rows // 8, 8, depth), axis=0))

    lane = lax.broadcasted_iota(jnp.int32, (1, depth), 1)
    peak_row = jnp.zeros((1, depth), jnp.float32)
    blocks = rows // z_rows
    steps = tile_y // 2 // blocks
    done = None
    for level in (3, 2, 1, 0, None):
        best = jnp.zeros((8, depth), jnp.float32)
        for c in range(blocks):
            if level is not None:
                for yp in range(steps * c, steps * (c + 1)):
                    x_step(level, yp)
            if done is not None:
                best = z_step(done, c, best)
        if done is not None:
            peak_row = jnp.where(lane == done, jnp.max(best), peak_row)
        done = level
    peaks[...] = peak_row


def score_kernel(stats, all_peaks, throat, flat):
    peaks = jnp.max(all_peaks[...], axis=0, keepdims=True)
    spreads = [0.25 * peaks[:, level : level + 1] + 1e-06 for level in range(4)]

    def body(c, carry):
        at = pl.ds(pl.multiple_of(c * 24, 24), 24)
        best = None
        for level, spread in enumerate(spreads):
            trace_sum = stats[3 * level, at, :]
            minors = stats[3 * level + 1, at, :]
            energy = stats[3 * level + 2, at, :]
            guard = energy + 0.1 * spread
            root = lax.rsqrt(guard)
            ratio = minors * root * root
            score = (
                (1.0 - jnp.exp2(energy * (-0.5 * log2_e / spread)))
                * jnp.exp2(ratio * ratio * (-2.0 * log2_e))
                * (1.0 - jnp.tanh(2.0 * trace_sum * root))
            )
            best = score if best is None else jnp.maximum(best, score)
        flat[at, :] = 0.5 * best
        return carry

    lax.fori_loop(0, rows // 24, body, 0, unroll=32)
    for i in range(tile_x):
        throat[i] = flat[pl.ds(i, tile_y, stride=tile_x), :]


def vmem(n):
    return [pl.BlockSpec(memory_space=pltpu.VMEM)] * n


def early_call(odd, volume, mid_near, mid_wrap, weights, interpret=False):
    return pl.pallas_call(
        early_kernel,
        out_shape=[jax.ShapeDtypeStruct((tile_x * pitch, depth), jnp.float32)] * 4,
        in_specs=[pl.BlockSpec(memory_space=pltpu.SMEM)] + vmem(6),
        out_specs=vmem(4),
        compiler_params=pltpu.CompilerParams(vmem_limit_bytes=16 * mib),
        interpret=interpret,
    )(odd, volume, *weights, mid_near, mid_wrap)


def late_call(core, odd, weights, pieces, early, interpret=False):
    return pl.pallas_call(
        late_kernel,
        out_shape=(
            jax.ShapeDtypeStruct((12, rows, depth), jnp.float32),
            jax.ShapeDtypeStruct((1, depth), jnp.float32),
        ),
        in_specs=[pl.BlockSpec(memory_space=pltpu.SMEM)] * 2 + vmem(13),
        out_specs=tuple(vmem(2)),
        scratch_shapes=[
            pltpu.VMEM(((count - tile_x) * pitch, depth), jnp.float32) for count in planes
        ]
        + [pltpu.VMEM((4, 6, rows, 2 * depth), jnp.bfloat16)],
        compiler_params=pltpu.CompilerParams(vmem_limit_bytes=28 * mib),
        interpret=interpret,
    )(core, odd, *weights, *pieces, *early)


def score_call(stats, peaks, interpret=False):
    return pl.pallas_call(
        score_kernel,
        out_shape=jax.ShapeDtypeStruct((tile_x, tile_y, depth), jnp.float32),
        in_specs=vmem(2),
        out_specs=vmem(1)[0],
        scratch_shapes=[pltpu.VMEM((rows, depth), jnp.float32)],
        compiler_params=pltpu.CompilerParams(vmem_limit_bytes=8 * mib),
        interpret=interpret,
    )(stats, peaks)


def all_peaks(row):
    axes = x_axes + y_axes
    peers = lax.axis_size(axes)
    spread = jnp.broadcast_to(row[None], (peers, 1, depth))
    return lax.all_to_all(spread, axes, 0, 0, tiled=True).reshape(peers, depth)


def per_device(volume):
    n_x, n_y = lax.axis_size(x_axes), lax.axis_size(y_axes)
    pair_perm = [(i, i ^ 1) for i in range(n_x)]
    far_perm = [(i, i + 1) for i in range(1, n_x - 1, 2)]
    far_perm += [(j, i) for i, j in far_perm]
    near_perm = [(i, i ^ 1) for i in range(n_y)]
    wrap_perm = [(i, i + 1) for i in range(1, n_y - 1, 2)]
    wrap_perm += [(j, i) for i, j in wrap_perm]

    odd = lax.axis_index("y") & 1
    core = lax.axis_index("core")
    volume, core, odd, is_odd, is_even = lax.optimization_barrier(
        (volume, core.reshape(1), odd.reshape(1), odd == 1, odd == 0)
    )

    def edge(tile, top):
        return jnp.where(top, tile[:, tile_y - rim :], tile[:, :rim])

    far = lax.ppermute(volume, x_axes, far_perm)
    mid_wrap = lax.ppermute(edge(volume, is_odd), y_axes, wrap_perm)
    mid_near = lax.ppermute(edge(volume, is_even), y_axes, near_perm)
    pair = lax.ppermute(volume, x_axes, pair_perm)
    far_wrap, far_near = edge(far, is_odd), edge(far, is_even)
    _, _, mid_wrap, mid_near = lax.optimization_barrier((far_wrap, far_near, mid_wrap, mid_near))
    far_wrap = lax.ppermute(far_wrap, y_axes, wrap_perm)
    far_near = lax.ppermute(far_near, y_axes, near_perm)
    weights = [jnp.asarray(w) for w in constants()]
    early = early_call(odd, volume, mid_near, mid_wrap, weights)
    pair_near = lax.ppermute(mid_near, x_axes, pair_perm)
    pair_wrap = lax.ppermute(mid_wrap, x_axes, pair_perm)
    pieces = (far, far_near, far_wrap, pair, pair_near, pair_wrap)
    stats, peaks = late_call(core, odd, weights, pieces, early)
    return score_call(stats, all_peaks(peaks))


def solution(mesh):
    fine = jax.sharding.Mesh(
        mesh.devices.reshape(4, 2, 4, 2, 4), ("zh", "core", "x", "zl", "y")
    )
    spec = P(x_axes, y_axes, None)
    return jax.shard_map(
        per_device, mesh=fine, in_specs=(spec,), out_specs=spec, check_vma=False
    )
```
